32 devices in a mesh: dp: 8 (over z, y), bn: 4 (over x, core).
Axes of the slice: x: 2, y: 2, z: 4, core: 2. Of those that a mesh axis runs over, the one named last changes fastest.
Arguments:
- key_feats: bfloat16 [256, 12, 16, 2048], P(('dp', 'bn')), may hold values from -22 to 22
- clip_starts: int32 [256], P(('dp', 'bn')), may hold values from 0 to 4
- shuffle: int32 [4, 8], P('bn'), may hold values from 0 to 7, each once within a row
- query_feats: bfloat16 [256, 2048], P(('dp', 'bn')), may hold values from -6 to 6
- conv_time: bfloat16 [3, 2048, 512], replicated, may hold values from -0.078125 to 0.078125
- conv_space: bfloat16 [9, 512, 512], replicated, may hold values from -0.09375 to 0.09375
- conv_expand: bfloat16 [512, 2048], replicated, may hold values from -0.25 to 0.25
- gain_one: float32 [512], replicated, may hold values from 0.25 to 1.75
- shift_one: float32 [512], replicated, may hold values from -3 to 3
- gain_two: float32 [512], replicated, may hold values from 0.25 to 1.75
- shift_two: float32 [512], replicated, may hold values from -3 to 3
- gain_three: float32 [2048], replicated, may hold values from 0.25 to 1.75
- shift_three: float32 [2048], replicated, may hold values from -3 to 3
- w_key: bfloat16 [2048, 128], replicated, may hold values from -0.125 to 0.125
- w_query: bfloat16 [2048, 128], replicated, may hold values from -0.125 to 0.125
- queue: bfloat16 [16384, 128], replicated, may hold values from -6 to 6
Outputs:
- keys: bfloat16 [256, 128], P(('dp', 'bn'))
- query_grad: float32 [2048, 128], replicated
The draws below stay inside these ranges and needn't reach their ends.
Inputs may be any that keep to these rules, and one draw needn't show every extreme that they name: `shuffle`: each row is a permutation of 0 to 7.
All inputs are finite; a program needn't handle non-finite values.
Results may differ from the reference program's by a relative error of at most 0.0061.
Values may be sent and summed in bfloat16 or wider, within the bound.
No kernel may reach another device: no remote copies, remote signals or barrier semaphores. Data moves between devices by JAX's collectives and lax.ppermute only.
A program may use at most 128 MiB of HBM per device.

```python
import jax
import jax.numpy as jnp
from jax import lax

C = 2048
INNER = 512
EMB = 128
QUEUE = 16384
FRAMES = 8
SIDE = 4
TF = 12
CLIP_DEV = 8
SPOTS = 16
PEERS = 8
GROUPS = 4
CLIPS = 256


def draw_key_feats(key, part):
    base_key = jax.random.fold_in(key, 11)
    random_key, scale_key = jax.random.split(base_key, 2)
    extent = (CLIPS, TF, SPOTS, C)
    random_part = jnp.clip(jax.random.normal(random_key, extent, jnp.float32), -6.0, 6.0)
    clip_scale = jnp.exp(jax.random.uniform(scale_key, (CLIPS,), jnp.float32, jnp.log(0.5), jnp.log(2.0)))
    member = jnp.arange(CLIPS) // CLIP_DEV % GROUPS
    ramp_factor = 1.0 + 0.8 * member.astype(jnp.float32) / max(GROUPS - 1, 1)
    return (random_part * (clip_scale * ramp_factor)[:, None, None, None]).astype(jnp.bfloat16)


def set_ends(array, key, least, high):
    place = [jax.random.randint(jax.random.fold_in(key, axis), (), 0, length) for axis, length in enumerate(array.shape)]
    widest = array.shape.index(max(array.shape))
    next_to = place[:widest] + [(place[widest] + 1) % array.shape[widest]] + place[widest + 1:]
    return array.at[tuple(place)].set(least).at[tuple(next_to)].set(high)


def block_scale(stream_key, shape, pieces, smallest, largest):
    factor_of, own = 1.0, jax.random.fold_in(stream_key, 6)
    for position, shards_of in pieces:
        heights = jnp.exp(jax.random.uniform(jax.random.fold_in(own, position), (shards_of,), jnp.float32, smallest / len(pieces), largest / len(pieces)))
        factor_of = factor_of * jnp.repeat(heights, shape[position] // shards_of).reshape([-1 if axis == position else 1 for axis in range(len(shape))])
    return factor_of


def normal_values(rng, dims, width, limit, cuts=(), kind=jnp.bfloat16):
    entries = width * jax.random.normal(rng, dims, jnp.float32)
    if cuts:
        entries = entries * block_scale(rng, dims, cuts, -0.22, 0.18)
    return jnp.clip(entries, -limit, limit).astype(kind)


def setup_inputs(seed: int = 0) -> dict:
    key_list = jax.random.split(jax.random.key(seed), 17)
    key_feats = draw_key_feats(jax.random.fold_in(key_list[16], 71), 0)
    clip_starts = set_ends(jax.random.randint(key_list[1], (CLIPS,), 0, TF - FRAMES + 1), jax.random.fold_in(key_list[1], 1), 0, TF - FRAMES).astype(jnp.int32)
    shuffle = jax.vmap(lambda own: jax.random.permutation(own, PEERS))(jax.random.split(key_list[2], GROUPS)).reshape((GROUPS, PEERS)).astype(jnp.int32)
    query_feats = normal_values(key_list[3], (CLIPS, C), 1.0, 6.0, ((0, 32),))
    conv_time = normal_values(key_list[4], (3, C, INNER), (3 * C) ** -0.5, 0.078125)
    conv_space = normal_values(key_list[5], (9, INNER, INNER), (9 * INNER) ** -0.5, 0.09375)
    conv_expand = normal_values(key_list[6], (INNER, C), INNER ** -0.5, 0.25)
    gain_one = jnp.clip(1.0 + 0.15 * jax.random.normal(key_list[7], (INNER,), jnp.float32), 0.25, 1.75)
    shift_one = normal_values(key_list[8], (INNER,), 0.5, 3.0, (), jnp.float32)
    gain_two = jnp.clip(1.0 + 0.15 * jax.random.normal(key_list[9], (INNER,), jnp.float32), 0.25, 1.75)
    shift_two = normal_values(key_list[10], (INNER,), 0.5, 3.0, (), jnp.float32)
    gain_three = jnp.clip(1.0 + 0.15 * jax.random.normal(key_list[11], (C,), jnp.float32), 0.25, 1.75)
    shift_three = normal_values(key_list[12], (C,), 0.5, 3.0, (), jnp.float32)
    w_key = normal_values(key_list[13], (C, EMB), C ** -0.5, 0.125)
    w_query = normal_values(key_list[14], (C, EMB), C ** -0.5, 0.125)
    queue = normal_values(key_list[15], (QUEUE, EMB), 1.0, 6.0)
    return dict(key_feats=key_feats, clip_starts=clip_starts, shuffle=shuffle, query_feats=query_feats, conv_time=conv_time, conv_space=conv_space, conv_expand=conv_expand, gain_one=gain_one, shift_one=shift_one, gain_two=gain_two, shift_two=shift_two, gain_three=gain_three, shift_three=shift_three, w_key=w_key, w_query=w_query, queue=queue)


SHARPNESS_DIVISOR = 0.2
EPSILON = 1e-05

def pick_frames(features, starts):

    def single(clip_feats, first_frame):
        return lax.dynamic_slice_in_dim(clip_feats, first_frame, FRAMES, 0)
    return jax.vmap(single)(features, starts.astype(jnp.int32))

def time_conv(values, weights):
    padded = jnp.pad(values.astype(jnp.float32), ((0, 0), (1, 1), (0, 0), (0, 0)))
    length = values.shape[1]
    summed = jnp.zeros(values.shape[:3] + (weights.shape[2],), jnp.float32)
    for offset in range(3):
        summed = summed + jnp.einsum('afsc,cd->afsd', padded[:, offset:offset + length], weights[offset].astype(jnp.float32))
    return summed

def space_conv(values, weights):
    square_grid = values.astype(jnp.float32).reshape(values.shape[0], values.shape[1], SIDE, SIDE, values.shape[3])
    padded = jnp.pad(square_grid, ((0, 0), (0, 0), (1, 1), (1, 1), (0, 0)))
    summed = jnp.zeros((values.shape[0], values.shape[1], SIDE, SIDE, weights.shape[2]), jnp.float32)
    for row_shift in range(3):
        for col_shift in range(3):
            window = padded[:, :, row_shift:row_shift + SIDE, col_shift:col_shift + SIDE]
            summed = summed + jnp.einsum('afhwc,cd->afhwd', window, weights[3 * row_shift + col_shift].astype(jnp.float32))
    return summed.reshape(values.shape[0], values.shape[1], SIDE * SIDE, weights.shape[2])

def batch_norm(values, total_sum, squares, row_count, gain_row, shift_row):
    center = total_sum / row_count
    spread = squares / row_count - center * center
    return (values - center) * (gain_row * lax.rsqrt(spread + EPSILON)) + shift_row

def local_moments(values):
    return (lax.optimization_barrier(jnp.sum(values, axis=(0, 1, 2))), lax.optimization_barrier(jnp.sum(values * values, axis=(0, 1, 2))))

def encode(values, params, moments, row_count):
    conv_time, conv_space, conv_expand, gain_one, shift_one, gain_two, shift_two, gain_three, shift_three, w_key = params
    first_out = time_conv(values, conv_time)
    total_sum, squares = moments(first_out)
    act_one = jnp.maximum(batch_norm(first_out, total_sum, squares, row_count, gain_one, shift_one), 0.0).astype(jnp.bfloat16)
    second = space_conv(act_one, conv_space)
    total_sum, squares = moments(second)
    act_two = jnp.maximum(batch_norm(second, total_sum, squares, row_count, gain_two, shift_two), 0.0).astype(jnp.bfloat16)
    third_out = jnp.einsum('afsc,cd->afsd', act_two.astype(jnp.float32), conv_expand.astype(jnp.float32))
    total_sum, squares = moments(third_out)
    merged = jnp.maximum(batch_norm(third_out, total_sum, squares, row_count, gain_three, shift_three) + values.astype(jnp.float32), 0.0)
    pooled = lax.optimization_barrier(jnp.mean(merged, axis=(1, 2))).astype(jnp.bfloat16)
    projected = jnp.dot(pooled, w_key, preferred_element_type=jnp.float32)
    return (projected * lax.rsqrt(lax.optimization_barrier(jnp.sum(projected * projected, axis=-1, keepdims=True)) + 1e-06)).astype(jnp.bfloat16)

def query_terms(query_feats, own_keys, w_query, queue):
    projected = jnp.dot(query_feats, w_query, preferred_element_type=jnp.float32)
    length = jnp.sqrt(lax.optimization_barrier(jnp.sum(projected * projected, axis=-1, keepdims=True)) + 1e-06)
    anchor_direction = projected / length
    queue_wide = queue.astype(jnp.float32)
    memory_bank_directions = (queue_wide * lax.rsqrt(lax.optimization_barrier(jnp.sum(queue_wide * queue_wide, axis=-1, keepdims=True)) + 1e-06)).astype(jnp.bfloat16)
    collected_encodings = own_keys.astype(jnp.float32)
    matching_scores = lax.optimization_barrier(jnp.sum(anchor_direction * collected_encodings, axis=-1)) / SHARPNESS_DIVISOR
    distractor_scores = jnp.einsum('nf,ef->ne', anchor_direction.astype(jnp.bfloat16).astype(jnp.float32), memory_bank_directions.astype(jnp.float32)) / SHARPNESS_DIVISOR
    partition = jnp.exp(matching_scores) + lax.optimization_barrier(jnp.sum(jnp.exp(distractor_scores), axis=-1))
    log_total = jnp.log(partition)
    weight_pos = jnp.exp(matching_scores - log_total)
    weight_neg = jnp.exp(distractor_scores - log_total[:, None]).astype(jnp.bfloat16)
    retrieved_samples = jnp.dot(weight_neg, memory_bank_directions, preferred_element_type=jnp.float32) + (weight_pos - 1.0)[:, None] * collected_encodings
    anchor_loss_derivative = retrieved_samples / SHARPNESS_DIVISOR
    radial = lax.optimization_barrier(jnp.sum(anchor_direction * anchor_loss_derivative, axis=-1, keepdims=True))
    grad_proj = ((anchor_loss_derivative - radial * anchor_direction) / length).astype(jnp.bfloat16)
    return jnp.einsum('nc,ne->ce', query_feats.astype(jnp.float32), grad_proj.astype(jnp.float32))

def reference(key_feats, clip_starts, shuffle, query_feats, conv_time, conv_space, conv_expand, gain_one, shift_one, gain_two, shift_two, gain_three, shift_three, w_key, w_query, queue):
    params = (conv_time, conv_space, conv_expand, gain_one, shift_one, gain_two, shift_two, gain_three, shift_three, w_key)
    positions = jnp.arange(PEERS, dtype=jnp.int32)
    matches = (shuffle[:, :, None] == positions[None, None, :]).astype(jnp.int32)
    inverse = lax.optimization_barrier(jnp.sum(positions[None, :, None] * matches, axis=1)).astype(jnp.int32)

    def group_keys(host_group):
        members = []
        for member in range(GROUPS):
            source = inverse[member, host_group]
            first_clip = ((source * GROUPS + member) * CLIP_DEV).astype(jnp.int32)
            clip_feats = lax.dynamic_slice_in_dim(key_feats, first_clip, CLIP_DEV, 0)
            starts = lax.dynamic_slice_in_dim(clip_starts, first_clip, CLIP_DEV, 0)
            members.append(pick_frames(clip_feats, starts))
        values = jnp.concatenate(members, axis=0)
        row_count = values.shape[0] * values.shape[1] * values.shape[2]
        encoded = encode(values, params, local_moments, row_count)
        return encoded.reshape(GROUPS, CLIP_DEV, EMB)
    hosted = lax.map(group_keys, positions)
    returned = jnp.stack([jnp.take(hosted[:, member], shuffle[member], axis=0) for member in range(GROUPS)], axis=1)
    own_keys = returned.reshape(CLIPS, EMB)
    query_grad = query_terms(query_feats, own_keys, w_query, queue)
    return (own_keys, query_grad)
```

```python
import jax
import jax.numpy as jnp
from jax import lax
from jax.sharding import PartitionSpec as P

FRAMES = 8
SIDE = 4


SHARPNESS_DIVISOR = 0.2
EPSILON = 1e-05


def pick_frames(features, starts):

    def single(clip_feats, first_frame):
        return lax.dynamic_slice_in_dim(clip_feats, first_frame, FRAMES, 0)

    return jax.vmap(single)(features, starts)


def time_conv(values, weights):
    padded = jnp.pad(values, ((0, 0), (1, 1), (0, 0), (0, 0)))
    length = values.shape[1]
    summed = jnp.zeros(values.shape[:3] + (weights.shape[2],), jnp.float32)
    for offset in range(3):
        summed = summed + jnp.einsum(
            "afsc,cd->afsd",
            padded[:, offset : offset + length],
            weights[offset],
            preferred_element_type=jnp.float32,
        )
    return summed


def space_conv(values, weights):
    square_grid = values.reshape(values.shape[0], values.shape[1], SIDE, SIDE, values.shape[3])
    padded = jnp.pad(square_grid, ((0, 0), (0, 0), (1, 1), (1, 1), (0, 0)))
    summed = jnp.zeros(
        (values.shape[0], values.shape[1], SIDE, SIDE, weights.shape[2]), jnp.float32
    )
    for row_shift in range(3):
        for col_shift in range(3):
            window = padded[:, :, row_shift : row_shift + SIDE, col_shift : col_shift + SIDE]
            summed = summed + jnp.einsum(
                "afhwc,cd->afhwd",
                window,
                weights[3 * row_shift + col_shift],
                preferred_element_type=jnp.float32,
            )
    return summed.reshape(values.shape[0], values.shape[1], SIDE * SIDE, weights.shape[2])


def batch_norm(values, total_sum, squares, row_count, gain_row, shift_row):
    center = total_sum / row_count
    spread = squares / row_count - center * center
    return (values - center) * (gain_row * lax.rsqrt(spread + EPSILON)) + shift_row


def encode(values, params, moments, row_count):
    (
        conv_time,
        conv_space,
        conv_expand,
        gain_one,
        shift_one,
        gain_two,
        shift_two,
        gain_three,
        shift_three,
        w_key,
    ) = params
    first_out = time_conv(values, conv_time)
    total_sum, squares = moments(first_out)
    act_one = jnp.maximum(
        batch_norm(first_out, total_sum, squares, row_count, gain_one, shift_one), 0.0
    ).astype(jnp.bfloat16)
    second = space_conv(act_one, conv_space)
    total_sum, squares = moments(second)
    act_two = jnp.maximum(
        batch_norm(second, total_sum, squares, row_count, gain_two, shift_two), 0.0
    ).astype(jnp.bfloat16)
    third_out = jnp.einsum(
        "afsc,cd->afsd", act_two, conv_expand, preferred_element_type=jnp.float32
    )
    total_sum, squares = moments(third_out)
    merged = jnp.maximum(
        batch_norm(third_out, total_sum, squares, row_count, gain_three, shift_three)
        + values.astype(jnp.float32),
        0.0,
    )
    pooled = jnp.mean(merged, axis=(1, 2)).astype(jnp.bfloat16)
    projected = jnp.dot(pooled, w_key, preferred_element_type=jnp.float32)
    return (
        projected * lax.rsqrt(jnp.sum(projected * projected, axis=-1, keepdims=True) + 1e-06)
    ).astype(jnp.bfloat16)


def query_terms(query_feats, own_keys, w_query, queue):
    projected = jnp.dot(query_feats, w_query, preferred_element_type=jnp.float32)
    length = jnp.sqrt(jnp.sum(projected * projected, axis=-1, keepdims=True) + 1e-06)
    anchor_direction = projected / length
    queue_wide = queue.astype(jnp.float32)
    memory_bank_directions = (
        queue_wide * lax.rsqrt(jnp.sum(queue_wide * queue_wide, axis=-1, keepdims=True) + 1e-06)
    ).astype(jnp.bfloat16)
    collected_encodings = own_keys.astype(jnp.float32)
    matching_scores = jnp.sum(anchor_direction * collected_encodings, axis=-1) / SHARPNESS_DIVISOR
    distractor_scores = (
        jnp.einsum(
            "nf,ef->ne",
            anchor_direction.astype(jnp.bfloat16),
            memory_bank_directions,
            preferred_element_type=jnp.float32,
        )
        / SHARPNESS_DIVISOR
    )
    partition = jnp.exp(matching_scores) + jnp.sum(jnp.exp(distractor_scores), axis=-1)
    log_total = jnp.log(partition)
    weight_pos = jnp.exp(matching_scores - log_total)
    weight_neg = jnp.exp(distractor_scores - log_total[:, None]).astype(jnp.bfloat16)
    retrieved_samples = (
        jnp.dot(weight_neg, memory_bank_directions, preferred_element_type=jnp.float32)
        + (weight_pos - 1.0)[:, None] * collected_encodings
    )
    anchor_loss_derivative = retrieved_samples / SHARPNESS_DIVISOR
    radial = jnp.sum(anchor_direction * anchor_loss_derivative, axis=-1, keepdims=True)
    return ((anchor_loss_derivative - radial * anchor_direction) / length).astype(jnp.bfloat16)


def spread_to_all(own):
    device_count = lax.axis_size("dp") * lax.axis_size("bn")
    copies = jnp.broadcast_to(own[None], (device_count,) + own.shape)
    return lax.all_to_all(copies, ("dp", "bn"), 0, 0)


def local(
    key_feats,
    clip_starts,
    shuffle,
    query_feats,
    conv_time,
    conv_space,
    conv_expand,
    gain_one,
    shift_one,
    gain_two,
    shift_two,
    gain_three,
    shift_three,
    w_key,
    w_query,
    queue,
):
    params = (
        conv_time,
        conv_space,
        conv_expand,
        gain_one,
        shift_one,
        gain_two,
        shift_two,
        gain_three,
        shift_three,
        w_key,
    )
    chosen = pick_frames(key_feats, clip_starts)
    peer_count = lax.axis_size("dp")
    groups = lax.axis_size("bn")
    target = shuffle[0, lax.axis_index("dp")]
    row_count = groups * chosen.shape[0] * chosen.shape[1] * chosen.shape[2]
    tables = lax.all_gather(shuffle[0], "bn")
    same = (tables.T == target).astype(jnp.float32).reshape(peer_count * groups, 1)
    all_queries = lax.all_gather(query_feats, ("dp", "bn"))

    def table_moments(values):
        width = values.shape[-1]
        own = jnp.concatenate(
            [jnp.sum(values, axis=(0, 1, 2)), jnp.sum(values * values, axis=(0, 1, 2))]
        )
        every = spread_to_all(own.reshape(-1, 128)).reshape(peer_count * groups, 2 * width)
        total = jnp.sum(every * same, axis=0)
        return total[:width], total[width:]

    own_keys = encode(chosen, params, table_moments, row_count)
    grad_proj = query_terms(query_feats, own_keys, w_query, queue)
    all_grads = spread_to_all(grad_proj)
    query_grad = jnp.einsum(
        "dnc,dne->ce", all_queries, all_grads, preferred_element_type=jnp.float32
    )
    return (own_keys, query_grad)


def solution(mesh):
    placed = (
        P(("dp", "bn"), None, None, None),
        P(("dp", "bn")),
        P("bn", None),
        P(("dp", "bn"), None),
        P(),
        P(),
        P(),
        P(),
        P(),
        P(),
        P(),
        P(),
        P(),
        P(),
        P(),
        P(),
    )
    return jax.shard_map(
        local, mesh=mesh, in_specs=placed, out_specs=(P(("dp", "bn"), None), P()), check_vma=False
    )
```

```python
import functools

import jax
import jax.numpy as jnp
from jax import lax
from jax.experimental import pallas as pl
from jax.experimental.pallas import tpu as pltpu
from jax.sharding import PartitionSpec as P

FRAMES = 8
SIDE = 4
SPOTS = SIDE * SIDE
LANES = 128
SHARPNESS_DIVISOR = 0.2
EPSILON = 1e-05
MIB = 1 << 20

VMEM = pl.BlockSpec(memory_space=pltpu.VMEM)
ANY = pl.BlockSpec(memory_space=pl.ANY)


def in_hbm(array):
    return pltpu.with_memory_space_constraint(array, pltpu.HBM)


def as_row(block):
    return jnp.concatenate([block[i : i + 1] for i in range(block.shape[0])], axis=1)


def as_block(row):
    return jnp.concatenate(
        [row[:, i : i + LANES] for i in range(0, row.shape[1], LANES)], axis=0
    )


def two_halves(values):
    high = values.astype(jnp.bfloat16).astype(jnp.float32)
    return high, values - high


def mean_and_var(total, squares, count):
    mean = total / count
    return mean, jnp.maximum(squares / count - mean * mean, 0.0)


def write_moments(message, mean, var, group):
    high, low = two_halves(mean)
    part = [as_block(high), as_block(low), as_block(var)]
    rest = message.shape[1] - sum(p.shape[0] for p in part)
    part.append(jnp.broadcast_to(group, (rest, LANES)))
    block = jnp.concatenate(part, axis=0).astype(jnp.bfloat16)
    message[...] = jnp.broadcast_to(block[None], message.shape)


def group_row(message, part):
    return message[0, 3 * part : 3 * part + 1, :].astype(jnp.float32)


def members(message, group, part):
    sender = message[:, 3 * part : 3 * part + 1, :].astype(jnp.float32)
    return (sender == group[None]).astype(jnp.float32)


def group_scale_and_bias(message, group, gain, shift):
    part = gain.shape[1] // LANES
    same = members(message, group, part)
    every = message[...].astype(jnp.float32)
    block_mean = every[:, :part] + every[:, part : 2 * part]
    block_var = every[:, 2 * part : 3 * part]
    blocks = jnp.sum(same, axis=0)
    mean = jnp.sum(block_mean * same, axis=0) / blocks
    apart = block_mean - mean[None]
    var = jnp.sum((block_var + apart * apart) * same, axis=0) / blocks
    scale = gain[...] * lax.rsqrt(as_row(var) + EPSILON)
    return scale, shift[...] - as_row(mean) * scale


def time_conv_kernel(
    cuts,
    starts_hbm,
    shuffle_hbm,
    feats,
    weights,
    first,
    frames,
    message,
    starts,
    shuffle,
    taps,
    small_sem,
    frames_sem,
    taps_sem,
):
    clips, _, spots, _ = feats.shape
    inner = weights.shape[2]
    pieces = len(cuts) - 1
    rows = clips * FRAMES * spots
    span = [pl.ds(cuts[k], cuts[k + 1] - cuts[k]) for k in range(pieces)]

    def copy_clip(k, n):
        return pltpu.make_async_copy(
            feats.at[n, pl.ds(starts[n], FRAMES), :, span[k]],
            frames.at[n, pl.ds(1, FRAMES), :, span[k]],
            frames_sem.at[k, n],
        )

    def copy_taps(k):
        return pltpu.make_async_copy(
            weights.at[:, span[k], :], taps.at[:, span[k], :], taps_sem.at[k]
        )

    copy_starts = pltpu.make_async_copy(starts_hbm, starts, small_sem.at[0])
    copy_shuffle = pltpu.make_async_copy(shuffle_hbm, shuffle, small_sem.at[1])
    copy_starts.start()
    copy_shuffle.start()
    copy_taps(0).start()
    copy_starts.wait()
    for k in range(pieces):
        for n in range(clips):
            copy_clip(k, n).start()
        if k + 1 < pieces:
            copy_taps(k + 1).start()
    blank = jnp.zeros((clips, 1) + frames.shape[2:], jnp.bfloat16)
    frames[:, 0:1] = blank
    frames[:, FRAMES + 1 : FRAMES + 2] = blank
    for k in range(pieces):
        depth = cuts[k + 1] - cuts[k]
        copy_taps(k).wait()
        for n in range(clips):
            copy_clip(k, n).wait()
        stacked = jnp.concatenate(
            [
                frames[:, o : o + FRAMES, :, cuts[k] : cuts[k + 1]].reshape(rows, depth)
                for o in range(3)
            ],
            axis=1,
        )
        product = jnp.dot(
            stacked,
            taps[:, cuts[k] : cuts[k + 1], :].reshape(3 * depth, inner),
            preferred_element_type=jnp.float32,
        )
        for j in range(inner // LANES):
            piece = product[:, j * LANES : (j + 1) * LANES]
            if k == 0:
                first[j] = piece
            else:
                first[j] += piece
    total, squares = [], []
    for j in range(inner // LANES):
        values = first[j]
        total.append(jnp.sum(values, axis=0, keepdims=True))
        squares.append(jnp.sum(values * values, axis=0, keepdims=True))
    mean, var = mean_and_var(
        jnp.concatenate(total, axis=1), jnp.concatenate(squares, axis=1), rows
    )
    copy_shuffle.wait()
    group = shuffle[0, lax.axis_index("dp")].astype(jnp.float32)
    write_moments(message, mean, var, jnp.full((1, LANES), group, jnp.float32))


def space_conv_kernel(own, got, gain, shift, first, weights, second, message, act, taken):
    inner = weights.shape[1]
    part = inner // LANES
    rows = first.shape[1] // SPOTS
    number = group_row(own, part)
    scale, bias = group_scale_and_bias(got, number, gain, shift)
    for r in range(SIDE):
        for c in range(SIDE):
            values = jnp.concatenate(
                [first[j, pl.ds(r * SIDE + c, rows, stride=SPOTS), :] for j in range(part)],
                axis=1,
            )
            act[r, c] = jnp.maximum(values * scale + bias, 0.0).astype(jnp.bfloat16)
    for k in (4, 0, 1, 2, 3, 5, 6, 7, 8):
        down, right = k // 3 - 1, k % 3 - 1
        r0, r1 = max(0, -down), min(SIDE, SIDE - down)
        c0, c1 = max(0, -right), min(SIDE, SIDE - right)
        source = act[r0 + down : r1 + down, c0 + right : c1 + right]
        product = jnp.dot(
            source.reshape((r1 - r0) * (c1 - c0) * rows, inner),
            weights[k],
            preferred_element_type=jnp.float32,
        ).reshape(r1 - r0, c1 - c0, rows, inner)
        if k == 4:
            taken[...] = product
        else:
            taken[r0:r1, c0:c1] += product
    total = jnp.zeros((1, inner), jnp.float32)
    squares = jnp.zeros((1, inner), jnp.float32)
    for r in range(SIDE):
        for c in range(SIDE):
            values = taken[r, c]
            for j in range(part):
                second[j, r * SIDE + c, 0:rows] = values[:, j * LANES : (j + 1) * LANES]
            total = total + jnp.sum(values, axis=0, keepdims=True)
            squares = squares + jnp.sum(values * values, axis=0, keepdims=True)
    mean, var = mean_and_var(total, squares, rows * SPOTS)
    write_moments(message, mean, var, number)


def expand_kernel(own, got, gain, shift, second, weights, third, message, act):
    inner, channels = weights.shape
    rows = act.shape[0]
    part = inner // LANES
    scale, bias = group_scale_and_bias(got, group_row(own, part), gain, shift)
    pitch = second.shape[1] // SPOTS
    total = jnp.zeros((SPOTS, inner), jnp.float32)
    for i in range(rows // SPOTS):
        values = jnp.concatenate(
            [second[j, pl.ds(i, SPOTS, stride=pitch), :] for j in range(part)], axis=1
        )
        act_two = jnp.maximum(values * scale + bias, 0.0).astype(jnp.bfloat16)
        act[i * SPOTS : (i + 1) * SPOTS] = act_two
        total = total + act_two.astype(jnp.float32)
    act_mean = jnp.sum(total, axis=0, keepdims=True) / rows
    high, low = two_halves(act_mean)
    found = []
    width = 4 * LANES
    for start in range(0, channels, width):
        product = jnp.dot(
            act[...], weights[:, start : start + width], preferred_element_type=jnp.float32
        )
        for j in range(width // LANES):
            third[start // LANES + j] = product[:, j * LANES : (j + 1) * LANES]
        total = jnp.sum(product, axis=0, keepdims=True)
        squares = jnp.sum(product * product, axis=0, keepdims=True)
        found.append(mean_and_var(total, squares, rows)[1])
    var = jnp.concatenate(found, axis=1)
    block = jnp.concatenate([as_block(high), as_block(low), as_block(var)], axis=0)
    message[...] = jnp.broadcast_to(block.astype(jnp.bfloat16)[None], message.shape)


def keys_kernel(
    own_numbers,
    numbers,
    got,
    gain,
    shift,
    weights,
    third,
    w_key,
    unit,
    length,
    negatives,
    pulled,
    frames,
    keys,
    message,
    pooled,
):
    clips = frames.shape[0]
    inner, channels = weights.shape
    part, wide = inner // LANES, channels // LANES
    same = members(numbers, group_row(own_numbers, part), part)
    act_mean = jnp.concatenate(
        [
            jnp.concatenate([got[:, h * part + j, :] for j in range(part)], axis=1)
            for h in range(2)
        ],
        axis=0,
    )
    parts = jnp.dot(act_mean, weights[...], preferred_element_type=jnp.float32)
    devices = got.shape[0]
    block_mean = parts[:devices] + parts[devices:]
    chosen = same[:, 0, 0:1]
    blocks = jnp.sum(same, axis=0)
    mean = jnp.sum(block_mean * chosen, axis=0, keepdims=True) / blocks[:, 0:1]
    apart = block_mean - mean
    between = jnp.sum(apart * apart * chosen, axis=0, keepdims=True) / blocks[:, 0:1]
    block_var = got[:, 2 * part : 2 * part + wide, :].astype(jnp.float32)
    within = as_row(jnp.sum(block_var * same, axis=0) / blocks)
    scale = gain[...] * lax.rsqrt(within + between + EPSILON)
    bias = shift[...] - mean * scale

    def one_clip(n, _):
        total = jnp.zeros((SPOTS, channels), jnp.float32)
        for t in range(FRAMES):
            values = jnp.concatenate(
                [
                    third[j, pl.ds((n * FRAMES + t) * SPOTS, SPOTS), :]
                    for j in range(wide)
                ],
                axis=1,
            )
            total = total + jnp.maximum(
                values * scale + bias + frames[n, t + 1].astype(jnp.float32), 0.0
            )
        pooled[pl.ds(n, 1), :] = jnp.sum(total, axis=0, keepdims=True) / (FRAMES * SPOTS)
        return 0

    lax.fori_loop(0, clips, one_clip, 0)
    projected = jnp.dot(
        pooled[...].astype(jnp.bfloat16), w_key[...], preferred_element_type=jnp.float32
    )
    own = (
        projected * lax.rsqrt(jnp.sum(projected * projected, axis=-1, keepdims=True) + 1e-06)
    ).astype(jnp.bfloat16)
    keys[...] = own
    own = own.astype(jnp.float32)
    direction = unit[...]
    positive = jnp.exp(jnp.sum(direction * own, axis=-1, keepdims=True) / SHARPNESS_DIVISOR)
    partition = positive + negatives[...]
    grad = (pulled[...] / partition + (positive / partition - 1.0) * own) / SHARPNESS_DIVISOR
    radial = jnp.sum(direction * grad, axis=-1, keepdims=True)
    grad = ((grad - radial * direction) / length[...]).astype(jnp.bfloat16)
    message[...] = jnp.broadcast_to(grad[None], message.shape)


def queue_kernel(query_feats, w_query, queue, unit, length, negatives, pulled):
    projected = jnp.dot(query_feats[...], w_query[...], preferred_element_type=jnp.float32)
    norm = jnp.sqrt(jnp.sum(projected * projected, axis=-1, keepdims=True) + 1e-06)
    direction = projected / norm
    unit[...] = direction
    length[...] = jnp.broadcast_to(norm, length.shape)
    rounded = direction.astype(jnp.bfloat16)
    rows, width = rounded.shape
    ones = jnp.ones((rows, width), jnp.bfloat16)
    across = (((1,), (1,)), ((), ()))
    step = queue.shape[0] // 8

    def one_step(i, carry):
        total, weighted = carry
        entries = queue[pl.ds(i * step, step), :]
        squares = lax.dot_general(
            ones, entries * entries, across, preferred_element_type=jnp.float32
        )
        inverse = lax.rsqrt(squares + 1e-06)
        scores = lax.dot_general(rounded, entries, across, preferred_element_type=jnp.float32)
        weight = jnp.exp(scores * inverse / SHARPNESS_DIVISOR)
        total = total + jnp.sum(weight, axis=-1, keepdims=True)
        weighted = weighted + jnp.dot(
            (weight * inverse).astype(jnp.bfloat16), entries, preferred_element_type=jnp.float32
        )
        return total, weighted

    total, weighted = lax.fori_loop(
        0,
        8,
        one_step,
        (jnp.zeros((rows, 1), jnp.float32), jnp.zeros((rows, width), jnp.float32)),
    )
    negatives[...] = jnp.broadcast_to(total, negatives.shape)
    pulled[...] = weighted


def gradient_kernel(queries_hbm, grads, out_hbm, queries, out, queries_sem, out_sem):
    channels = out.shape[0]
    width = channels // queries_sem.shape[0]

    def fetch(i):
        span = pl.ds(i * width, width)
        return pltpu.make_async_copy(
            queries_hbm.at[:, span], queries.at[:, span], queries_sem.at[i]
        )

    def give(i):
        span = pl.ds(i * width, width)
        return pltpu.make_async_copy(out.at[span], out_hbm.at[span], out_sem.at[i])

    pieces = channels // width
    for i in range(pieces):
        fetch(i).start()
    for i in range(pieces):
        fetch(i).wait()
        out[i * width : (i + 1) * width] = lax.dot_general(
            queries[:, i * width : (i + 1) * width],
            grads[...],
            (((0,), (0,)), ((), ())),
            preferred_element_type=jnp.float32,
        )
        give(i).start()
    for i in range(pieces):
        give(i).wait()


def exchange(message):
    return lax.all_to_all(message, ("dp", "bn"), 0, 0)


def local(
    key_feats,
    clip_starts,
    shuffle,
    query_feats,
    conv_time,
    conv_space,
    conv_expand,
    gain_one,
    shift_one,
    gain_two,
    shift_two,
    gain_three,
    shift_three,
    w_key,
    w_query,
    queue,
):
    devices = lax.axis_size("dp") * lax.axis_size("bn")
    clips, _, spots, channels = key_feats.shape
    inner, emb = conv_space.shape[1], queue.shape[1]
    part, wide = inner // LANES, channels // LANES
    rows = clips * FRAMES * spots
    short = jax.ShapeDtypeStruct((devices, 16, LANES), jnp.bfloat16)
    row = lambda vector: vector.reshape(1, -1)

    all_queries = lax.all_gather(query_feats, ("dp", "bn"), tiled=True)

    cuts = (0, channels // 8, 3 * channels // 8, channels)
    pieces = len(cuts) - 1
    padded = (clips, FRAMES + 2, spots, channels)
    first, frames, sent_one = pl.pallas_call(
        functools.partial(time_conv_kernel, cuts),
        out_shape=(
            jax.ShapeDtypeStruct((part, rows, LANES), jnp.float32),
            jax.ShapeDtypeStruct(padded, jnp.bfloat16),
            short,
        ),
        in_specs=[ANY] * 4,
        out_specs=(VMEM,) * 3,
        scratch_shapes=[
            pltpu.SMEM(clip_starts.shape, jnp.int32),
            pltpu.SMEM(shuffle.shape, jnp.int32),
            pltpu.VMEM(conv_time.shape, jnp.bfloat16),
            pltpu.SemaphoreType.DMA((2,)),
            pltpu.SemaphoreType.DMA((pieces, clips)),
            pltpu.SemaphoreType.DMA((pieces,)),
        ],
        compiler_params=pltpu.CompilerParams(vmem_limit_bytes=20 * MIB),
        name="time_conv",
    )(in_hbm(clip_starts), in_hbm(shuffle), in_hbm(key_feats), in_hbm(conv_time))
    got_one = exchange(sent_one)

    unit, length, negatives, pulled = pl.pallas_call(
        queue_kernel,
        out_shape=(jax.ShapeDtypeStruct((clips, emb), jnp.float32),) * 4,
        in_specs=[VMEM] * 3,
        out_specs=(VMEM,) * 4,
        compiler_params=pltpu.CompilerParams(vmem_limit_bytes=4 * MIB),
        name="queue_terms",
    )(query_feats, w_query, queue)

    grid_rows = rows // spots
    pitch = grid_rows + 8
    second, sent_two = pl.pallas_call(
        space_conv_kernel,
        out_shape=(jax.ShapeDtypeStruct((part, SPOTS, pitch, LANES), jnp.float32), short),
        in_specs=[VMEM] * 6,
        out_specs=(VMEM, VMEM),
        scratch_shapes=[
            pltpu.VMEM((SIDE, SIDE, grid_rows, inner), jnp.bfloat16),
            pltpu.VMEM((SIDE, SIDE, grid_rows, inner), jnp.float32),
        ],
        compiler_params=pltpu.CompilerParams(vmem_limit_bytes=10 * MIB),
        name="space_conv",
    )(sent_one, got_one, row(gain_one), row(shift_one), first, conv_space)
    got_two = exchange(sent_two)
    second = second.reshape(part, SPOTS * pitch, LANES)

    third, sent = pl.pallas_call(
        expand_kernel,
        out_shape=(
            jax.ShapeDtypeStruct((wide, rows, LANES), jnp.float32),
            jax.ShapeDtypeStruct((devices, 2 * part + wide, LANES), jnp.bfloat16),
        ),
        in_specs=[VMEM] * 6,
        out_specs=(VMEM, VMEM),
        scratch_shapes=[pltpu.VMEM((rows, inner), jnp.bfloat16)],
        compiler_params=pltpu.CompilerParams(vmem_limit_bytes=8 * MIB),
        name="expand",
    )(sent_two, got_two, row(gain_two), row(shift_two), second, conv_expand)
    got_three = exchange(sent)

    own_keys, sent = pl.pallas_call(
        keys_kernel,
        out_shape=(
            jax.ShapeDtypeStruct((clips, emb), jnp.bfloat16),
            jax.ShapeDtypeStruct((devices, clips, emb), jnp.bfloat16),
        ),
        in_specs=[VMEM] * 13,
        out_specs=(VMEM, VMEM),
        scratch_shapes=[pltpu.VMEM((clips, channels), jnp.float32)],
        compiler_params=pltpu.CompilerParams(vmem_limit_bytes=8 * MIB),
        name="keys",
    )(
        sent_one,
        got_one,
        got_three,
        row(gain_three),
        row(shift_three),
        conv_expand,
        third,
        w_key,
        unit,
        length,
        negatives,
        pulled,
        frames,
    )
    all_grads = exchange(sent).reshape(devices * clips, emb)
    query_grad = pl.pallas_call(
        gradient_kernel,
        out_shape=jax.ShapeDtypeStruct((channels, emb), jnp.float32),
        in_specs=[ANY, VMEM],
        out_specs=ANY,
        scratch_shapes=[
            pltpu.VMEM(all_queries.shape, jnp.bfloat16),
            pltpu.VMEM((channels, emb), jnp.float32),
            pltpu.SemaphoreType.DMA((4,)),
            pltpu.SemaphoreType.DMA((4,)),
        ],
        compiler_params=pltpu.CompilerParams(vmem_limit_bytes=12 * MIB),
        name="query_grad",
    )(in_hbm(all_queries), all_grads)
    return (own_keys, query_grad)


def solution(mesh):
    both = ("dp", "bn")
    placed = (
        P(both, None, None, None),
        P(both),
        P("bn", None),
        P(both, None),
    ) + (P(),) * 12
    return jax.shard_map(
        local, mesh=mesh, in_specs=placed, out_specs=(P(both, None), P()), check_vma=False
    )
```

```python
import functools

import jax
import jax.numpy as jnp
from jax import lax
from jax.experimental import pallas as pl
from jax.experimental.pallas import tpu as pltpu
from jax.sharding import PartitionSpec as P

FRAMES = 8
SIDE = 4
SPOTS = SIDE * SIDE
LANES = 128
SHARPNESS_DIVISOR = 0.2
EPSILON = 1e-05
MIB = 1 << 20
MOMENT_ROWS = 16
QUERY_ROWS = 16

VMEM = pl.BlockSpec(memory_space=pltpu.VMEM)
ANY = pl.BlockSpec(memory_space=pl.ANY)


def in_hbm(array):
    return pltpu.with_memory_space_constraint(array, pltpu.HBM)


def as_row(block):
    return jnp.concatenate([block[i : i + 1] for i in range(block.shape[0])], axis=1)


def as_block(row):
    return jnp.concatenate(
        [row[:, i : i + LANES] for i in range(0, row.shape[1], LANES)], axis=0
    )


def write_queries(message, query_feats, piece):
    half = query_feats.shape[1] // 2
    parts = []
    for side in range(2):
        at = side * half + piece * 2 * LANES
        parts.append(
            jnp.concatenate(
                [query_feats[:, at : at + LANES], query_feats[:, at + LANES : at + 2 * LANES]],
                axis=0,
            )
        )
    pair = jnp.stack(parts)
    devices, length, _ = message.shape
    every = jnp.broadcast_to(pair[None], (devices // 2,) + pair.shape)
    message[:, length - pair.shape[1] :, :] = every.reshape((devices,) + pair.shape[1:])


def two_halves(values):
    high = values.astype(jnp.bfloat16).astype(jnp.float32)
    return high, values - high


def mean_and_var(total, squares, count):
    mean = total / count
    return mean, jnp.maximum(squares / count - mean * mean, 0.0)


def write_moments(message, mean, var, group):
    high, low = two_halves(mean)
    part = [as_block(high), as_block(low), as_block(var)]
    rest = MOMENT_ROWS - sum(p.shape[0] for p in part)
    part.append(jnp.broadcast_to(group, (rest, LANES)))
    block = jnp.concatenate(part, axis=0).astype(jnp.bfloat16)
    message[:, :MOMENT_ROWS, :] = jnp.broadcast_to(block[None], (message.shape[0],) + block.shape)


def group_row(message, part):
    return message[0, 3 * part : 3 * part + 1, :].astype(jnp.float32)


def members(message, group, part):
    sender = message[:, 3 * part : 3 * part + 1, :].astype(jnp.float32)
    return (sender == group[None]).astype(jnp.float32)


def group_scale_and_bias(message, group, gain, shift):
    part = gain.shape[1] // LANES
    same = members(message, group, part)
    every = message[:, :MOMENT_ROWS, :].astype(jnp.float32)
    block_mean = every[:, :part] + every[:, part : 2 * part]
    block_var = every[:, 2 * part : 3 * part]
    blocks = jnp.sum(same, axis=0)
    mean = jnp.sum(block_mean * same, axis=0) / blocks
    apart = block_mean - mean[None]
    var = jnp.sum((block_var + apart * apart) * same, axis=0) / blocks
    scale = gain[...] * lax.rsqrt(as_row(var) + EPSILON)
    return scale, shift[...] - as_row(mean) * scale


def time_conv_kernel(
    cuts,
    starts_hbm,
    shuffle_hbm,
    feats,
    weights,
    queries_hbm,
    first,
    frames,
    message,
    starts,
    shuffle,
    query_feats,
    taps,
    small_sem,
    frames_sem,
    taps_sem,
):
    clips, _, spots, _ = feats.shape
    inner = weights.shape[2]
    pieces = len(cuts) - 1
    rows = clips * FRAMES * spots
    span = [pl.ds(cuts[k], cuts[k + 1] - cuts[k]) for k in range(pieces)]

    def copy_clip(k, n):
        return pltpu.make_async_copy(
            feats.at[n, pl.ds(starts[n], FRAMES), :, span[k]],
            frames.at[n, pl.ds(1, FRAMES), :, span[k]],
            frames_sem.at[k, n],
        )

    def copy_taps(k):
        return pltpu.make_async_copy(
            weights.at[:, span[k], :], taps.at[:, span[k], :], taps_sem.at[k]
        )

    copy_starts = pltpu.make_async_copy(starts_hbm, starts, small_sem.at[0])
    copy_shuffle = pltpu.make_async_copy(shuffle_hbm, shuffle, small_sem.at[1])
    copy_queries = pltpu.make_async_copy(queries_hbm, query_feats, small_sem.at[2])
    copy_starts.start()
    copy_shuffle.start()
    copy_taps(0).start()
    copy_starts.wait()
    for k in range(pieces):
        for n in range(clips):
            copy_clip(k, n).start()
        if k + 1 < pieces:
            copy_taps(k + 1).start()
    copy_queries.start()
    blank = jnp.zeros((clips, 1) + frames.shape[2:], jnp.bfloat16)
    frames[:, 0:1] = blank
    frames[:, FRAMES + 1 : FRAMES + 2] = blank
    for k in range(pieces):
        depth = cuts[k + 1] - cuts[k]
        copy_taps(k).wait()
        for n in range(clips):
            copy_clip(k, n).wait()
        stacked = jnp.concatenate(
            [
                frames[:, o : o + FRAMES, :, cuts[k] : cuts[k + 1]].reshape(rows, depth)
                for o in range(3)
            ],
            axis=1,
        )
        product = jnp.dot(
            stacked,
            taps[:, cuts[k] : cuts[k + 1], :].reshape(3 * depth, inner),
            preferred_element_type=jnp.float32,
        )
        for j in range(inner // LANES):
            piece = product[:, j * LANES : (j + 1) * LANES]
            if k == 0:
                first[j] = piece
            else:
                first[j] += piece
    total, squares = [], []
    for j in range(inner // LANES):
        values = first[j]
        total.append(jnp.sum(values, axis=0, keepdims=True))
        squares.append(jnp.sum(values * values, axis=0, keepdims=True))
    mean, var = mean_and_var(
        jnp.concatenate(total, axis=1), jnp.concatenate(squares, axis=1), rows
    )
    copy_shuffle.wait()
    group = shuffle[0, lax.axis_index("dp")].astype(jnp.float32)
    write_moments(message, mean, var, jnp.full((1, LANES), group, jnp.float32))
    copy_queries.wait()
    write_queries(message, query_feats, 0)


def space_conv_kernel(
    own, got, gain, shift, first, weights, query_feats, second, message, act, taken
):
    inner = weights.shape[1]
    part = inner // LANES
    rows = first.shape[1] // SPOTS
    number = group_row(own, part)
    scale, bias = group_scale_and_bias(got, number, gain, shift)
    for r in range(SIDE):
        for c in range(SIDE):
            values = jnp.concatenate(
                [first[j, pl.ds(r * SIDE + c, rows, stride=SPOTS), :] for j in range(part)],
                axis=1,
            )
            act[r, c] = jnp.maximum(values * scale + bias, 0.0).astype(jnp.bfloat16)
    for k in (4, 0, 1, 2, 3, 5, 6, 7, 8):
        down, right = k // 3 - 1, k % 3 - 1
        r0, r1 = max(0, -down), min(SIDE, SIDE - down)
        c0, c1 = max(0, -right), min(SIDE, SIDE - right)
        source = act[r0 + down : r1 + down, c0 + right : c1 + right]
        product = jnp.dot(
            source.reshape((r1 - r0) * (c1 - c0) * rows, inner),
            weights[k],
            preferred_element_type=jnp.float32,
        ).reshape(r1 - r0, c1 - c0, rows, inner)
        if k == 4:
            taken[...] = product
        else:
            taken[r0:r1, c0:c1] += product
    total = jnp.zeros((1, inner), jnp.float32)
    squares = jnp.zeros((1, inner), jnp.float32)
    for r in range(SIDE):
        for c in range(SIDE):
            values = taken[r, c]
            for j in range(part):
                second[j, r * SIDE + c, 0:rows] = values[:, j * LANES : (j + 1) * LANES]
            total = total + jnp.sum(values, axis=0, keepdims=True)
            squares = squares + jnp.sum(values * values, axis=0, keepdims=True)
    mean, var = mean_and_var(total, squares, rows * SPOTS)
    write_moments(message, mean, var, number)
    write_queries(message, query_feats, 1)


def expand_kernel(own, got, gain, shift, second, weights, query_feats, third, message, act):
    inner, channels = weights.shape
    rows = act.shape[0]
    part = inner // LANES
    scale, bias = group_scale_and_bias(got, group_row(own, part), gain, shift)
    pitch = second.shape[1] // SPOTS
    total = jnp.zeros((SPOTS, inner), jnp.float32)
    for i in range(rows // SPOTS):
        values = jnp.concatenate(
            [second[j, pl.ds(i, SPOTS, stride=pitch), :] for j in range(part)], axis=1
        )
        act_two = jnp.maximum(values * scale + bias, 0.0).astype(jnp.bfloat16)
        act[i * SPOTS : (i + 1) * SPOTS] = act_two
        total = total + act_two.astype(jnp.float32)
    act_mean = jnp.sum(total, axis=0, keepdims=True) / rows
    high, low = two_halves(act_mean)
    found = []
    width = 4 * LANES
    for start in range(0, channels, width):
        product = jnp.dot(
            act[...], weights[:, start : start + width], preferred_element_type=jnp.float32
        )
        for j in range(width // LANES):
            third[start // LANES + j] = product[:, j * LANES : (j + 1) * LANES]
        total = jnp.sum(product, axis=0, keepdims=True)
        squares = jnp.sum(product * product, axis=0, keepdims=True)
        found.append(mean_and_var(total, squares, rows)[1])
    var = jnp.concatenate(found, axis=1)
    block = jnp.concatenate([as_block(high), as_block(low), as_block(var)], axis=0)
    block = block.astype(jnp.bfloat16)
    message[:, : block.shape[0], :] = jnp.broadcast_to(
        block[None], (message.shape[0],) + block.shape
    )
    write_queries(message, query_feats, 2)


def keys_kernel(
    own_numbers,
    numbers,
    got,
    gain,
    shift,
    weights,
    third,
    w_key,
    unit,
    length,
    negatives,
    pulled,
    frames,
    query_feats,
    keys,
    message,
    pooled,
):
    clips = frames.shape[0]
    inner, channels = weights.shape
    part, wide = inner // LANES, channels // LANES
    same = members(numbers, group_row(own_numbers, part), part)
    act_mean = jnp.concatenate(
        [
            jnp.concatenate([got[:, h * part + j, :] for j in range(part)], axis=1)
            for h in range(2)
        ],
        axis=0,
    )
    parts = jnp.dot(act_mean, weights[...], preferred_element_type=jnp.float32)
    devices = got.shape[0]
    block_mean = parts[:devices] + parts[devices:]
    chosen = same[:, 0, 0:1]
    blocks = jnp.sum(same, axis=0)
    mean = jnp.sum(block_mean * chosen, axis=0, keepdims=True) / blocks[:, 0:1]
    apart = block_mean - mean
    between = jnp.sum(apart * apart * chosen, axis=0, keepdims=True) / blocks[:, 0:1]
    block_var = got[:, 2 * part : 2 * part + wide, :].astype(jnp.float32)
    within = as_row(jnp.sum(block_var * same, axis=0) / blocks)
    scale = gain[...] * lax.rsqrt(within + between + EPSILON)
    bias = shift[...] - mean * scale

    def one_clip(n, _):
        total = jnp.zeros((SPOTS, channels), jnp.float32)
        for t in range(FRAMES):
            values = jnp.concatenate(
                [
                    third[j, pl.ds((n * FRAMES + t) * SPOTS, SPOTS), :]
                    for j in range(wide)
                ],
                axis=1,
            )
            total = total + jnp.maximum(
                values * scale + bias + frames[n, t + 1].astype(jnp.float32), 0.0
            )
        pooled[pl.ds(n, 1), :] = jnp.sum(total, axis=0, keepdims=True) / (FRAMES * SPOTS)
        return 0

    lax.fori_loop(0, clips, one_clip, 0)
    projected = jnp.dot(
        pooled[...].astype(jnp.bfloat16), w_key[...], preferred_element_type=jnp.float32
    )
    own = (
        projected * lax.rsqrt(jnp.sum(projected * projected, axis=-1, keepdims=True) + 1e-06)
    ).astype(jnp.bfloat16)
    keys[...] = own
    own = own.astype(jnp.float32)
    direction = unit[...]
    positive = jnp.exp(jnp.sum(direction * own, axis=-1, keepdims=True) / SHARPNESS_DIVISOR)
    partition = positive + negatives[...]
    grad = (pulled[...] / partition + (positive / partition - 1.0) * own) / SHARPNESS_DIVISOR
    radial = jnp.sum(direction * grad, axis=-1, keepdims=True)
    grad = ((grad - radial * direction) / length[...]).astype(jnp.bfloat16)
    message[:, :clips, :] = jnp.broadcast_to(grad[None], (message.shape[0],) + grad.shape)
    write_queries(message, query_feats, 3)


def queue_kernel(query_feats, w_query, queue, unit, length, negatives, pulled):
    projected = jnp.dot(query_feats[...], w_query[...], preferred_element_type=jnp.float32)
    norm = jnp.sqrt(jnp.sum(projected * projected, axis=-1, keepdims=True) + 1e-06)
    direction = projected / norm
    unit[...] = direction
    length[...] = jnp.broadcast_to(norm, length.shape)
    rounded = direction.astype(jnp.bfloat16)
    rows, width = rounded.shape
    none, ones = jnp.zeros((rows, width), jnp.bfloat16), jnp.ones((rows, width), jnp.bfloat16)
    both = jnp.concatenate(
        [jnp.concatenate([rounded, none], axis=1), jnp.concatenate([none, ones], axis=1)], axis=0
    )
    pieces = 8
    step = queue.shape[0] // pieces
    total = jnp.zeros((rows, 1), jnp.float32)
    weighted = jnp.zeros((rows, width), jnp.float32)
    for i in range(pieces):
        entries = queue[i * step : (i + 1) * step, :]
        products = lax.dot_general(
            both,
            jnp.concatenate([entries, entries * entries], axis=1),
            (((1,), (1,)), ((), ())),
            preferred_element_type=jnp.float32,
        )
        inverse = lax.rsqrt(products[rows:] + 1e-06)
        weight = jnp.exp(products[:rows] * inverse / SHARPNESS_DIVISOR)
        total = total + jnp.sum(weight, axis=-1, keepdims=True)
        weighted = weighted + jnp.dot(
            (weight * inverse).astype(jnp.bfloat16), entries, preferred_element_type=jnp.float32
        )
    negatives[...] = jnp.broadcast_to(total, negatives.shape)
    pulled[...] = weighted


def gradient_kernel(one, two, three, four, out):
    devices, _, width = four.shape
    clips = QUERY_ROWS // 2
    grads = four[:, :clips, :].reshape(devices * clips, width)
    for i, message in enumerate((one, two, three, four)):
        for j in range(2):
            at = message.shape[1] - QUERY_ROWS + j * clips
            queries = message[:, at : at + clips, :].reshape(devices * clips, LANES)
            start = (2 * i + j) * LANES
            out[start : start + LANES] = lax.dot_general(
                queries, grads, (((0,), (0,)), ((), ())), preferred_element_type=jnp.float32
            )


def exchange(message):
    return lax.all_to_all(message, ("dp", "bn"), 0, 0)


def local(
    key_feats,
    clip_starts,
    shuffle,
    query_feats,
    conv_time,
    conv_space,
    conv_expand,
    gain_one,
    shift_one,
    gain_two,
    shift_two,
    gain_three,
    shift_three,
    w_key,
    w_query,
    queue,
):
    devices = lax.axis_size("dp") * lax.axis_size("bn")
    clips, _, spots, channels = key_feats.shape
    inner, emb = conv_space.shape[1], queue.shape[1]
    part, wide = inner // LANES, channels // LANES
    rows = clips * FRAMES * spots
    short = jax.ShapeDtypeStruct((devices, MOMENT_ROWS + QUERY_ROWS, LANES), jnp.bfloat16)
    row = lambda vector: vector.reshape(1, -1)

    cuts = (0, channels // 8, 3 * channels // 8, channels)
    pieces = len(cuts) - 1
    padded = (clips, FRAMES + 2, spots, channels)
    first, frames, sent_one = pl.pallas_call(
        functools.partial(time_conv_kernel, cuts),
        out_shape=(
            jax.ShapeDtypeStruct((part, rows, LANES), jnp.float32),
            jax.ShapeDtypeStruct(padded, jnp.bfloat16),
            short,
        ),
        in_specs=[ANY] * 5,
        out_specs=(VMEM,) * 3,
        scratch_shapes=[
            pltpu.SMEM(clip_starts.shape, jnp.int32),
            pltpu.SMEM(shuffle.shape, jnp.int32),
            pltpu.VMEM(query_feats.shape, jnp.bfloat16),
            pltpu.VMEM(conv_time.shape, jnp.bfloat16),
            pltpu.SemaphoreType.DMA((3,)),
            pltpu.SemaphoreType.DMA((pieces, clips)),
            pltpu.SemaphoreType.DMA((pieces,)),
        ],
        compiler_params=pltpu.CompilerParams(vmem_limit_bytes=20 * MIB),
        name="time_conv",
    )(
        in_hbm(clip_starts),
        in_hbm(shuffle),
        in_hbm(key_feats),
        in_hbm(conv_time),
        in_hbm(query_feats),
    )
    late_queries, sent_one = lax.optimization_barrier((query_feats, sent_one))
    unit, length, negatives, pulled = pl.pallas_call(
        queue_kernel,
        out_shape=(jax.ShapeDtypeStruct((clips, emb), jnp.float32),) * 4,
        in_specs=[VMEM] * 3,
        out_specs=(VMEM,) * 4,
        compiler_params=pltpu.CompilerParams(vmem_limit_bytes=4 * MIB),
        name="queue_terms",
    )(late_queries, w_query, queue)
    sent_one, unit, length, negatives, pulled = lax.optimization_barrier(
        (sent_one, unit, length, negatives, pulled)
    )
    got_one = exchange(sent_one)

    grid_rows = rows // spots
    pitch = grid_rows + 8
    second, sent_two = pl.pallas_call(
        space_conv_kernel,
        out_shape=(jax.ShapeDtypeStruct((part, SPOTS, pitch, LANES), jnp.float32), short),
        in_specs=[VMEM] * 7,
        out_specs=(VMEM, VMEM),
        scratch_shapes=[
            pltpu.VMEM((SIDE, SIDE, grid_rows, inner), jnp.bfloat16),
            pltpu.VMEM((SIDE, SIDE, grid_rows, inner), jnp.float32),
        ],
        compiler_params=pltpu.CompilerParams(vmem_limit_bytes=10 * MIB),
        name="space_conv",
    )(sent_one, got_one, row(gain_one), row(shift_one), first, conv_space, query_feats)
    got_two = exchange(sent_two)
    second = second.reshape(part, SPOTS * pitch, LANES)

    third, sent = pl.pallas_call(
        expand_kernel,
        out_shape=(
            jax.ShapeDtypeStruct((wide, rows, LANES), jnp.float32),
            jax.ShapeDtypeStruct((devices, 2 * part + wide + QUERY_ROWS, LANES), jnp.bfloat16),
        ),
        in_specs=[VMEM] * 7,
        out_specs=(VMEM, VMEM),
        scratch_shapes=[pltpu.VMEM((rows, inner), jnp.bfloat16)],
        compiler_params=pltpu.CompilerParams(vmem_limit_bytes=8 * MIB),
        name="expand",
    )(sent_two, got_two, row(gain_two), row(shift_two), second, conv_expand, query_feats)
    got_three = exchange(sent)

    own_keys, sent = pl.pallas_call(
        keys_kernel,
        out_shape=(
            jax.ShapeDtypeStruct((clips, emb), jnp.bfloat16),
            jax.ShapeDtypeStruct((devices, clips + QUERY_ROWS, emb), jnp.bfloat16),
        ),
        in_specs=[VMEM] * 14,
        out_specs=(VMEM, VMEM),
        scratch_shapes=[pltpu.VMEM((clips, channels), jnp.float32)],
        compiler_params=pltpu.CompilerParams(vmem_limit_bytes=8 * MIB),
        name="keys",
    )(
        sent_one,
        got_one,
        got_three,
        row(gain_three),
        row(shift_three),
        conv_expand,
        third,
        w_key,
        unit,
        length,
        negatives,
        pulled,
        frames,
        query_feats,
    )
    got_four = exchange(sent)
    own_half = pl.pallas_call(
        gradient_kernel,
        out_shape=jax.ShapeDtypeStruct((channels // 2, emb), jnp.float32),
        in_specs=[VMEM] * 4,
        out_specs=VMEM,
        compiler_params=pltpu.CompilerParams(vmem_limit_bytes=6 * MIB),
        name="query_grad",
    )(got_one, got_two, got_three, got_four)
    members_bn = lax.axis_size("bn")
    other_half = lax.ppermute(own_half, "bn", [(i, i ^ 1) for i in range(members_bn)])
    odd = lax.axis_index("bn") % 2 == 1
    query_grad = jnp.concatenate(
        [jnp.where(odd, other_half, own_half), jnp.where(odd, own_half, other_half)], axis=0
    )
    return (own_keys, query_grad)


def solution(mesh):
    both = ("dp", "bn")
    placed = (
        P(both, None, None, None),
        P(both),
        P("bn", None),
        P(both, None),
    ) + (P(),) * 12
    return jax.shard_map(
        local, mesh=mesh, in_specs=placed, out_specs=(P(both, None), P()), check_vma=False
    )
```

```python
import functools

import jax
import jax.numpy as jnp
from jax import lax
from jax.experimental import pallas as pl
from jax.experimental.pallas import tpu as pltpu
from jax.sharding import PartitionSpec as P

FRAMES = 8
SIDE = 4
SPOTS = SIDE * SIDE
LANES = 128
SHARPNESS_DIVISOR = 0.2
EPSILON = 1e-05
MIB = 1 << 20
MOMENT_ROWS = 16
QUERY_ROWS = 16

VMEM = pl.BlockSpec(memory_space=pltpu.VMEM)
ANY = pl.BlockSpec(memory_space=pl.ANY)


def in_hbm(array):
    return pltpu.with_memory_space_constraint(array, pltpu.HBM)


def as_row(block):
    return jnp.concatenate([block[i : i + 1] for i in range(block.shape[0])], axis=1)


def as_block(row):
    return jnp.concatenate(
        [row[:, i : i + LANES] for i in range(0, row.shape[1], LANES)], axis=0
    )


def write_queries(message, query_feats, piece):
    half = query_feats.shape[1] // 2
    parts = []
    for side in range(2):
        at = side * half + piece * 2 * LANES
        parts.append(
            jnp.concatenate(
                [query_feats[:, at : at + LANES], query_feats[:, at + LANES : at + 2 * LANES]],
                axis=0,
            )
        )
    pair = jnp.stack(parts)
    devices, length, _ = message.shape
    every = jnp.broadcast_to(pair[None], (devices // 2,) + pair.shape)
    message[:, length - pair.shape[1] :, :] = every.reshape((devices,) + pair.shape[1:])


def two_halves(values):
    high = values.astype(jnp.bfloat16).astype(jnp.float32)
    return high, values - high


def mean_and_var(total, squares, count):
    mean = total / count
    return mean, jnp.maximum(squares / count - mean * mean, 0.0)


def write_moments(message, mean, var, group):
    high, low = two_halves(mean)
    part = [as_block(high), as_block(low), as_block(var)]
    rest = MOMENT_ROWS - sum(p.shape[0] for p in part)
    part.append(jnp.broadcast_to(group, (rest, LANES)))
    block = jnp.concatenate(part, axis=0).astype(jnp.bfloat16)
    message[:, :MOMENT_ROWS, :] = jnp.broadcast_to(block[None], (message.shape[0],) + block.shape)


def group_row(message, part):
    return message[0, 3 * part : 3 * part + 1, :].astype(jnp.float32)


def members(message, group, part):
    sender = message[:, 3 * part : 3 * part + 1, :].astype(jnp.float32)
    return (sender == group[None]).astype(jnp.float32)


def group_scale_and_bias(message, group, gain, shift):
    part = gain.shape[1] // LANES
    same = members(message, group, part)
    every = message[:, :MOMENT_ROWS, :].astype(jnp.float32)
    block_mean = every[:, :part] + every[:, part : 2 * part]
    block_var = every[:, 2 * part : 3 * part]
    blocks = jnp.sum(same, axis=0)
    mean = jnp.sum(block_mean * same, axis=0) / blocks
    apart = block_mean - mean[None]
    var = jnp.sum((block_var + apart * apart) * same, axis=0) / blocks
    scale = gain[...] * lax.rsqrt(as_row(var) + EPSILON)
    return scale, shift[...] - as_row(mean) * scale


def time_conv_kernel(
    cuts,
    starts_hbm,
    shuffle_hbm,
    feats,
    weights,
    queries_hbm,
    first,
    frames,
    message,
    starts,
    shuffle,
    query_feats,
    taps,
    small_sem,
    frames_sem,
    taps_sem,
):
    clips, _, spots, _ = feats.shape
    inner = weights.shape[2]
    pieces = len(cuts) - 1
    rows = clips * FRAMES * spots
    span = [pl.ds(cuts[k], cuts[k + 1] - cuts[k]) for k in range(pieces)]

    def copy_clip(k, n):
        return pltpu.make_async_copy(
            feats.at[n, pl.ds(starts[n], FRAMES), :, span[k]],
            frames.at[n, pl.ds(1, FRAMES), :, span[k]],
            frames_sem.at[k, n],
        )

    def copy_taps(k):
        return pltpu.make_async_copy(
            weights.at[:, span[k], :], taps.at[:, span[k], :], taps_sem.at[k]
        )

    copy_starts = pltpu.make_async_copy(starts_hbm, starts, small_sem.at[0])
    copy_shuffle = pltpu.make_async_copy(shuffle_hbm, shuffle, small_sem.at[1])
    copy_queries = pltpu.make_async_copy(queries_hbm, query_feats, small_sem.at[2])
    copy_starts.start()
    copy_shuffle.start()
    copy_taps(0).start()
    copy_starts.wait()
    for k in range(pieces):
        for n in range(clips):
            copy_clip(k, n).start()
        if k + 1 < pieces:
            copy_taps(k + 1).start()
    copy_queries.start()
    blank = jnp.zeros((clips, 1) + frames.shape[2:], jnp.bfloat16)
    frames[:, 0:1] = blank
    frames[:, FRAMES + 1 : FRAMES + 2] = blank
    for k in range(pieces):
        depth = cuts[k + 1] - cuts[k]
        copy_taps(k).wait()
        for n in range(clips):
            copy_clip(k, n).wait()
        stacked = jnp.concatenate(
            [
                frames[:, o : o + FRAMES, :, cuts[k] : cuts[k + 1]].reshape(rows, depth)
                for o in range(3)
            ],
            axis=1,
        )
        product = jnp.dot(
            stacked,
            taps[:, cuts[k] : cuts[k + 1], :].reshape(3 * depth, inner),
            preferred_element_type=jnp.float32,
        )
        for j in range(inner // LANES):
            piece = product[:, j * LANES : (j + 1) * LANES]
            if k == 0:
                first[j] = piece
            else:
                first[j] += piece
    total, squares = [], []
    for j in range(inner // LANES):
        values = first[j]
        total.append(jnp.sum(values, axis=0, keepdims=True))
        squares.append(jnp.sum(values * values, axis=0, keepdims=True))
    mean, var = mean_and_var(
        jnp.concatenate(total, axis=1), jnp.concatenate(squares, axis=1), rows
    )
    copy_shuffle.wait()
    group = shuffle[0, lax.axis_index("dp")].astype(jnp.float32)
    write_moments(message, mean, var, jnp.full((1, LANES), group, jnp.float32))
    copy_queries.wait()
    write_queries(message, query_feats, 0)


def space_conv_kernel(
    own, got, gain, shift, first, weights, query_feats, second, message, act, taken
):
    inner = weights.shape[1]
    part = inner // LANES
    rows = first.shape[1] // SPOTS
    number = group_row(own, part)
    scale, bias = group_scale_and_bias(got, number, gain, shift)
    for r in range(SIDE):
        for c in range(SIDE):
            values = jnp.concatenate(
                [first[j, pl.ds(r * SIDE + c, rows, stride=SPOTS), :] for j in range(part)],
                axis=1,
            )
            act[r, c] = jnp.maximum(values * scale + bias, 0.0).astype(jnp.bfloat16)
    for k in (4, 0, 1, 2, 3, 5, 6, 7, 8):
        down, right = k // 3 - 1, k % 3 - 1
        r0, r1 = max(0, -down), min(SIDE, SIDE - down)
        c0, c1 = max(0, -right), min(SIDE, SIDE - right)
        source = act[r0 + down : r1 + down, c0 + right : c1 + right]
        product = jnp.dot(
            source.reshape((r1 - r0) * (c1 - c0) * rows, inner),
            weights[k],
            preferred_element_type=jnp.float32,
        ).reshape(r1 - r0, c1 - c0, rows, inner)
        if k == 4:
            taken[...] = product
        else:
            taken[r0:r1, c0:c1] += product
    total = jnp.zeros((1, inner), jnp.float32)
    squares = jnp.zeros((1, inner), jnp.float32)
    for r in range(SIDE):
        for c in range(SIDE):
            values = taken[r, c]
            for j in range(part):
                second[j, r * SIDE + c, 0:rows] = values[:, j * LANES : (j + 1) * LANES]
            total = total + jnp.sum(values, axis=0, keepdims=True)
            squares = squares + jnp.sum(values * values, axis=0, keepdims=True)
    mean, var = mean_and_var(total, squares, rows * SPOTS)
    write_moments(message, mean, var, number)
    write_queries(message, query_feats, 1)


def expand_kernel(own, got, gain, shift, second, weights, query_feats, third, message, act):
    inner, channels = weights.shape
    rows = act.shape[0]
    part = inner // LANES
    scale, bias = group_scale_and_bias(got, group_row(own, part), gain, shift)
    pitch = second.shape[1] // SPOTS
    total = jnp.zeros((SPOTS, inner), jnp.float32)
    for i in range(rows // SPOTS):
        values = jnp.concatenate(
            [second[j, pl.ds(i, SPOTS, stride=pitch), :] for j in range(part)], axis=1
        )
        act_two = jnp.maximum(values * scale + bias, 0.0).astype(jnp.bfloat16)
        act[i * SPOTS : (i + 1) * SPOTS] = act_two
        total = total + act_two.astype(jnp.float32)
    act_mean = jnp.sum(total, axis=0, keepdims=True) / rows
    high, low = two_halves(act_mean)
    found = []
    width = 4 * LANES
    for start in range(0, channels, width):
        product = jnp.dot(
            act[...], weights[:, start : start + width], preferred_element_type=jnp.float32
        )
        for j in range(width // LANES):
            third[start // LANES + j] = product[:, j * LANES : (j + 1) * LANES]
        total = jnp.sum(product, axis=0, keepdims=True)
        squares = jnp.sum(product * product, axis=0, keepdims=True)
        found.append(mean_and_var(total, squares, rows)[1])
    var = jnp.concatenate(found, axis=1)
    block = jnp.concatenate([as_block(high), as_block(low), as_block(var)], axis=0)
    block = block.astype(jnp.bfloat16)
    message[:, : block.shape[0], :] = jnp.broadcast_to(
        block[None], (message.shape[0],) + block.shape
    )
    write_queries(message, query_feats, 2)


def keys_kernel(
    own_numbers,
    numbers,
    got,
    gain,
    shift,
    weights,
    third,
    w_key,
    frames,
    query_feats,
    w_query,
    queue,
    keys,
    message,
    pooled,
    products,
):
    clips = frames.shape[0]
    emb = queue.shape[1]
    query = jnp.dot(query_feats[...], w_query[...], preferred_element_type=jnp.float32)
    length = jnp.sqrt(jnp.sum(query * query, axis=-1, keepdims=True) + 1e-06)
    direction = query / length
    rounded = direction.astype(jnp.bfloat16)
    none, ones = jnp.zeros((clips, emb), jnp.bfloat16), jnp.ones((clips, emb), jnp.bfloat16)
    both = jnp.concatenate(
        [jnp.concatenate([rounded, none], axis=1), jnp.concatenate([none, ones], axis=1)], axis=0
    )
    step = queue.shape[0] // clips

    def queue_products(i):
        entries = queue[pl.ds(i * step, step), :]
        return lax.dot_general(
            both,
            jnp.concatenate([entries, entries * entries], axis=1),
            (((1,), (1,)), ((), ())),
            preferred_element_type=jnp.float32,
        )

    products[...] = queue_products(0)
    inner, channels = weights.shape
    part, wide = inner // LANES, channels // LANES
    same = members(numbers, group_row(own_numbers, part), part)
    act_mean = jnp.concatenate(
        [
            jnp.concatenate([got[:, h * part + j, :] for j in range(part)], axis=1)
            for h in range(2)
        ],
        axis=0,
    )
    parts = jnp.dot(act_mean, weights[...], preferred_element_type=jnp.float32)
    devices = got.shape[0]
    block_mean = parts[:devices] + parts[devices:]
    chosen = same[:, 0, 0:1]
    blocks = jnp.sum(same, axis=0)
    mean = jnp.sum(block_mean * chosen, axis=0, keepdims=True) / blocks[:, 0:1]
    apart = block_mean - mean
    between = jnp.sum(apart * apart * chosen, axis=0, keepdims=True) / blocks[:, 0:1]
    block_var = got[:, 2 * part : 2 * part + wide, :].astype(jnp.float32)
    within = as_row(jnp.sum(block_var * same, axis=0) / blocks)
    scale = gain[...] * lax.rsqrt(within + between + EPSILON)
    bias = shift[...] - mean * scale

    def one_step(n, carry):
        negatives, pulled = carry
        inverse = lax.rsqrt(products[clips:] + 1e-06)
        weight = jnp.exp(products[:clips] * inverse / SHARPNESS_DIVISOR)
        negatives = negatives + jnp.sum(weight, axis=-1, keepdims=True)
        pulled = pulled + jnp.dot(
            (weight * inverse).astype(jnp.bfloat16),
            queue[pl.ds(n * step, step), :],
            preferred_element_type=jnp.float32,
        )
        products[...] = queue_products(jnp.minimum(n + 1, clips - 1))
        total = jnp.zeros((SPOTS, channels), jnp.float32)
        for t in range(FRAMES):
            values = jnp.concatenate(
                [
                    third[j, pl.ds((n * FRAMES + t) * SPOTS, SPOTS), :]
                    for j in range(wide)
                ],
                axis=1,
            )
            total = total + jnp.maximum(
                values * scale + bias + frames[n, t + 1].astype(jnp.float32), 0.0
            )
        pooled[pl.ds(n, 1), :] = jnp.sum(total, axis=0, keepdims=True) / (FRAMES * SPOTS)
        return negatives, pulled

    negatives, pulled = lax.fori_loop(
        0,
        clips,
        one_step,
        (jnp.zeros((clips, 1), jnp.float32), jnp.zeros((clips, emb), jnp.float32)),
        unroll=clips,
    )
    projected = jnp.dot(
        pooled[...].astype(jnp.bfloat16), w_key[...], preferred_element_type=jnp.float32
    )
    own = (
        projected * lax.rsqrt(jnp.sum(projected * projected, axis=-1, keepdims=True) + 1e-06)
    ).astype(jnp.bfloat16)
    keys[...] = own
    own = own.astype(jnp.float32)
    positive = jnp.exp(jnp.sum(direction * own, axis=-1, keepdims=True) / SHARPNESS_DIVISOR)
    partition = positive + negatives
    grad = (pulled / partition + (positive / partition - 1.0) * own) / SHARPNESS_DIVISOR
    radial = jnp.sum(direction * grad, axis=-1, keepdims=True)
    grad = ((grad - radial * direction) / length).astype(jnp.bfloat16)
    message[:, :clips, :] = jnp.broadcast_to(grad[None], (message.shape[0],) + grad.shape)
    write_queries(message, query_feats, 3)


def gradient_kernel(one, two, three, four, out):
    devices, _, width = four.shape
    clips = QUERY_ROWS // 2
    grads = four[:, :clips, :].reshape(devices * clips, width)
    for i, message in enumerate((one, two, three, four)):
        for j in range(2):
            at = message.shape[1] - QUERY_ROWS + j * clips
            queries = message[:, at : at + clips, :].reshape(devices * clips, LANES)
            start = (2 * i + j) * LANES
            out[start : start + LANES] = lax.dot_general(
                queries, grads, (((0,), (0,)), ((), ())), preferred_element_type=jnp.float32
            )


def exchange(message):
    return lax.all_to_all(message, ("dp", "bn"), 0, 0)


def local(
    key_feats,
    clip_starts,
    shuffle,
    query_feats,
    conv_time,
    conv_space,
    conv_expand,
    gain_one,
    shift_one,
    gain_two,
    shift_two,
    gain_three,
    shift_three,
    w_key,
    w_query,
    queue,
):
    devices = lax.axis_size("dp") * lax.axis_size("bn")
    clips, _, spots, channels = key_feats.shape
    inner, emb = conv_space.shape[1], queue.shape[1]
    part, wide = inner // LANES, channels // LANES
    rows = clips * FRAMES * spots
    short = jax.ShapeDtypeStruct((devices, MOMENT_ROWS + QUERY_ROWS, LANES), jnp.bfloat16)
    row = lambda vector: vector.reshape(1, -1)

    cuts = (0, channels // 8, 3 * channels // 8, channels)
    pieces = len(cuts) - 1
    padded = (clips, FRAMES + 2, spots, channels)
    first, frames, sent_one = pl.pallas_call(
        functools.partial(time_conv_kernel, cuts),
        out_shape=(
            jax.ShapeDtypeStruct((part, rows, LANES), jnp.float32),
            jax.ShapeDtypeStruct(padded, jnp.bfloat16),
            short,
        ),
        in_specs=[ANY] * 5,
        out_specs=(VMEM,) * 3,
        scratch_shapes=[
            pltpu.SMEM(clip_starts.shape, jnp.int32),
            pltpu.SMEM(shuffle.shape, jnp.int32),
            pltpu.VMEM(query_feats.shape, jnp.bfloat16),
            pltpu.VMEM(conv_time.shape, jnp.bfloat16),
            pltpu.SemaphoreType.DMA((3,)),
            pltpu.SemaphoreType.DMA((pieces, clips)),
            pltpu.SemaphoreType.DMA((pieces,)),
        ],
        compiler_params=pltpu.CompilerParams(vmem_limit_bytes=20 * MIB),
        name="time_conv",
    )(
        in_hbm(clip_starts),
        in_hbm(shuffle),
        in_hbm(key_feats),
        in_hbm(conv_time),
        in_hbm(query_feats),
    )
    got_one = exchange(sent_one)

    grid_rows = rows // spots
    pitch = grid_rows + 8
    second, sent_two = pl.pallas_call(
        space_conv_kernel,
        out_shape=(jax.ShapeDtypeStruct((part, SPOTS, pitch, LANES), jnp.float32), short),
        in_specs=[VMEM] * 7,
        out_specs=(VMEM, VMEM),
        scratch_shapes=[
            pltpu.VMEM((SIDE, SIDE, grid_rows, inner), jnp.bfloat16),
            pltpu.VMEM((SIDE, SIDE, grid_rows, inner), jnp.float32),
        ],
        compiler_params=pltpu.CompilerParams(vmem_limit_bytes=10 * MIB),
        name="space_conv",
    )(sent_one, got_one, row(gain_one), row(shift_one), first, conv_space, query_feats)
    got_two = exchange(sent_two)
    second = second.reshape(part, SPOTS * pitch, LANES)

    third, sent = pl.pallas_call(
        expand_kernel,
        out_shape=(
            jax.ShapeDtypeStruct((wide, rows, LANES), jnp.float32),
            jax.ShapeDtypeStruct((devices, 2 * part + wide + QUERY_ROWS, LANES), jnp.bfloat16),
        ),
        in_specs=[VMEM] * 7,
        out_specs=(VMEM, VMEM),
        scratch_shapes=[pltpu.VMEM((rows, inner), jnp.bfloat16)],
        compiler_params=pltpu.CompilerParams(vmem_limit_bytes=8 * MIB),
        name="expand",
    )(sent_two, got_two, row(gain_two), row(shift_two), second, conv_expand, query_feats)
    got_three = exchange(sent)

    own_keys, sent = pl.pallas_call(
        keys_kernel,
        out_shape=(
            jax.ShapeDtypeStruct((clips, emb), jnp.bfloat16),
            jax.ShapeDtypeStruct((devices, clips + QUERY_ROWS, emb), jnp.bfloat16),
        ),
        in_specs=[VMEM] * 12,
        out_specs=(VMEM, VMEM),
        scratch_shapes=[
            pltpu.VMEM((clips, channels), jnp.float32),
            pltpu.VMEM((2 * clips, queue.shape[0] // clips), jnp.float32),
        ],
        compiler_params=pltpu.CompilerParams(vmem_limit_bytes=8 * MIB),
        name="keys",
    )(
        sent_one,
        got_one,
        got_three,
        row(gain_three),
        row(shift_three),
        conv_expand,
        third,
        w_key,
        frames,
        query_feats,
        w_query,
        queue,
    )
    got_four = exchange(sent)
    own_half = pl.pallas_call(
        gradient_kernel,
        out_shape=jax.ShapeDtypeStruct((channels // 2, emb), jnp.float32),
        in_specs=[VMEM] * 4,
        out_specs=VMEM,
        compiler_params=pltpu.CompilerParams(vmem_limit_bytes=6 * MIB),
        name="query_grad",
    )(got_one, got_two, got_three, got_four)
    members_bn = lax.axis_size("bn")
    other_half = lax.ppermute(own_half, "bn", [(i, i ^ 1) for i in range(members_bn)])
    odd = lax.axis_index("bn") % 2 == 1
    query_grad = jnp.concatenate(
        [jnp.where(odd, other_half, own_half), jnp.where(odd, own_half, other_half)], axis=0
    )
    return (own_keys, query_grad)


def solution(mesh):
    both = ("dp", "bn")
    placed = (
        P(both, None, None, None),
        P(both),
        P("bn", None),
        P(both, None),
    ) + (P(),) * 12
    return jax.shard_map(
        local, mesh=mesh, in_specs=placed, out_specs=(P(both, None), P()), check_vma=False
    )
```

```python
import functools

import jax
import jax.numpy as jnp
from jax import lax
from jax.experimental import pallas as pl
from jax.experimental.pallas import tpu as pltpu
from jax.sharding import PartitionSpec as P

FRAMES = 8
SIDE = 4
SPOTS = SIDE * SIDE
LANES = 128
SHARPNESS_DIVISOR = 0.2
EPSILON = 1e-05
MIB = 1 << 20
MOMENT_ROWS = 16

VMEM = pl.BlockSpec(memory_space=pltpu.VMEM)
ANY = pl.BlockSpec(memory_space=pl.ANY)


def in_hbm(array):
    return pltpu.with_memory_space_constraint(array, pltpu.HBM)


def as_row(block):
    return jnp.concatenate([block[i : i + 1] for i in range(block.shape[0])], axis=1)


def as_block(row):
    return jnp.concatenate(
        [row[:, i : i + LANES] for i in range(0, row.shape[1], LANES)], axis=0
    )


def write_queries(message, query_feats, units):
    half = query_feats.shape[1] // 2
    pair = jnp.stack(
        [
            jnp.concatenate(
                [
                    query_feats[:, side * half + u * LANES : side * half + (u + 1) * LANES]
                    for u in units
                ],
                axis=0,
            )
            for side in range(2)
        ]
    )
    devices, length, _ = message.shape
    every = jnp.broadcast_to(pair[None], (devices // 2,) + pair.shape)
    message[:, length - pair.shape[1] :, :] = every.reshape((devices,) + pair.shape[1:])


def two_halves(values):
    high = values.astype(jnp.bfloat16).astype(jnp.float32)
    return high, values - high


def mean_and_var(total, squares, count):
    mean = total / count
    return mean, jnp.maximum(squares / count - mean * mean, 0.0)


def write_moments(message, mean, var, group):
    high, low = two_halves(mean)
    part = [as_block(high), as_block(low), as_block(var)]
    rest = MOMENT_ROWS - sum(p.shape[0] for p in part)
    part.append(jnp.broadcast_to(group, (rest, LANES)))
    block = jnp.concatenate(part, axis=0).astype(jnp.bfloat16)
    message[:, :MOMENT_ROWS, :] = jnp.broadcast_to(block[None], (message.shape[0],) + block.shape)


def group_row(message, part):
    return message[0, 3 * part : 3 * part + 1, :].astype(jnp.float32)


def members(message, group, part):
    sender = message[:, 3 * part : 3 * part + 1, :].astype(jnp.float32)
    return (sender == group[None]).astype(jnp.float32)


def group_scale_and_bias(message, group, gain, shift):
    part = gain.shape[1] // LANES
    same = members(message, group, part)
    every = message[:, :MOMENT_ROWS, :].astype(jnp.float32)
    block_mean = every[:, :part] + every[:, part : 2 * part]
    block_var = every[:, 2 * part : 3 * part]
    blocks = jnp.sum(same, axis=0)
    mean = jnp.sum(block_mean * same, axis=0) / blocks
    apart = block_mean - mean[None]
    var = jnp.sum((block_var + apart * apart) * same, axis=0) / blocks
    scale = gain[...] * lax.rsqrt(as_row(var) + EPSILON)
    return scale, shift[...] - as_row(mean) * scale


def time_conv_kernel(
    cuts,
    units,
    starts_hbm,
    shuffle_hbm,
    feats,
    weights,
    queries_hbm,
    first,
    frames,
    message,
    starts,
    shuffle,
    query_feats,
    taps,
    small_sem,
    frames_sem,
    taps_sem,
):
    clips, _, spots, _ = feats.shape
    inner = weights.shape[2]
    pieces = len(cuts) - 1
    rows = clips * FRAMES * spots
    span = [pl.ds(cuts[k], cuts[k + 1] - cuts[k]) for k in range(pieces)]

    def copy_clip(k, n):
        return pltpu.make_async_copy(
            feats.at[n, pl.ds(starts[n], FRAMES), :, span[k]],
            frames.at[n, pl.ds(1, FRAMES), :, span[k]],
            frames_sem.at[k, n],
        )

    def copy_taps(k):
        return pltpu.make_async_copy(
            weights.at[:, span[k], :], taps.at[:, span[k], :], taps_sem.at[k]
        )

    copy_starts = pltpu.make_async_copy(starts_hbm, starts, small_sem.at[0])
    copy_shuffle = pltpu.make_async_copy(shuffle_hbm, shuffle, small_sem.at[1])
    copy_queries = pltpu.make_async_copy(queries_hbm, query_feats, small_sem.at[2])
    copy_starts.start()
    copy_shuffle.start()
    copy_taps(0).start()
    copy_starts.wait()
    for k in range(pieces):
        for n in range(clips):
            copy_clip(k, n).start()
        if k + 1 < pieces:
            copy_taps(k + 1).start()
    copy_queries.start()
    blank = jnp.zeros((clips, 1) + frames.shape[2:], jnp.bfloat16)
    frames[:, 0:1] = blank
    frames[:, FRAMES + 1 : FRAMES + 2] = blank
    total, squares = [], []
    for k in range(pieces):
        depth = cuts[k + 1] - cuts[k]
        copy_taps(k).wait()
        for n in range(clips):
            copy_clip(k, n).wait()
        stacked = jnp.concatenate(
            [
                frames[:, o : o + FRAMES, :, cuts[k] : cuts[k + 1]].reshape(rows, depth)
                for o in range(3)
            ],
            axis=1,
        )
        product = jnp.dot(
            stacked,
            taps[:, cuts[k] : cuts[k + 1], :].reshape(3 * depth, inner),
            preferred_element_type=jnp.float32,
        )
        for j in range(inner // LANES):
            piece = product[:, j * LANES : (j + 1) * LANES]
            if k > 0:
                piece = piece + first[j, :rows]
            first[j, :rows] = piece
            if k == pieces - 1:
                total.append(jnp.sum(piece, axis=0, keepdims=True))
                squares.append(jnp.sum(piece * piece, axis=0, keepdims=True))
    mean, var = mean_and_var(
        jnp.concatenate(total, axis=1), jnp.concatenate(squares, axis=1), rows
    )
    copy_shuffle.wait()
    group = shuffle[0, lax.axis_index("dp")].astype(jnp.float32)
    write_moments(message, mean, var, jnp.full((1, LANES), group, jnp.float32))
    copy_queries.wait()
    write_queries(message, query_feats, units)


def space_conv_kernel(
    units, own, got, gain, shift, first, weights, query_feats, second, message, act, taken
):
    inner = weights.shape[1]
    part = inner // LANES
    rows = act.shape[2]
    number = group_row(own, part)
    scale, bias = group_scale_and_bias(got, number, gain, shift)
    for r in range(SIDE):
        for c in range(SIDE):
            values = jnp.concatenate(
                [first[j, pl.ds(r * SIDE + c, rows, stride=SPOTS), :] for j in range(part)],
                axis=1,
            )
            act[r, c] = jnp.maximum(values * scale + bias, 0.0).astype(jnp.bfloat16)
    for k in (4, 0, 1, 2, 3, 5, 6, 7, 8):
        down, right = k // 3 - 1, k % 3 - 1
        r0, r1 = max(0, -down), min(SIDE, SIDE - down)
        c0, c1 = max(0, -right), min(SIDE, SIDE - right)
        source = act[r0 + down : r1 + down, c0 + right : c1 + right]
        product = jnp.dot(
            source.reshape((r1 - r0) * (c1 - c0) * rows, inner),
            weights[k],
            preferred_element_type=jnp.float32,
        ).reshape(r1 - r0, c1 - c0, rows, inner)
        if k == 4:
            taken[...] = product
        else:
            taken[r0:r1, c0:c1] += product
    total = jnp.zeros((1, inner), jnp.float32)
    squares = jnp.zeros((1, inner), jnp.float32)
    for r in range(SIDE):
        for c in range(SIDE):
            values = taken[r, c]
            for j in range(part):
                second[j, r * SIDE + c, 0:rows] = values[:, j * LANES : (j + 1) * LANES]
            total = total + jnp.sum(values, axis=0, keepdims=True)
            squares = squares + jnp.sum(values * values, axis=0, keepdims=True)
    mean, var = mean_and_var(total, squares, rows * SPOTS)
    write_moments(message, mean, var, number)
    write_queries(message, query_feats, units)


def expand_kernel(
    units, own, got, gain, shift, second, weights, query_feats, third, message, act):
    inner, channels = weights.shape
    rows = act.shape[0]
    part = inner // LANES
    scale, bias = group_scale_and_bias(got, group_row(own, part), gain, shift)
    pitch = second.shape[1] // (SPOTS + 1)
    total = jnp.zeros((SPOTS, inner), jnp.float32)
    for i in range(rows // SPOTS):
        values = jnp.concatenate(
            [second[j, pl.ds(i, SPOTS, stride=pitch), :] for j in range(part)], axis=1
        )
        act_two = jnp.maximum(values * scale + bias, 0.0).astype(jnp.bfloat16)
        act[i * SPOTS : (i + 1) * SPOTS] = act_two
        total = total + act_two.astype(jnp.float32)
    act_mean = jnp.sum(total, axis=0, keepdims=True) / rows
    high, low = two_halves(act_mean)
    found = []
    width = 4 * LANES
    for start in range(0, channels, width):
        product = jnp.dot(
            act[...], weights[:, start : start + width], preferred_element_type=jnp.float32
        )
        for j in range(width // LANES):
            third[start // LANES + j] = product[:, j * LANES : (j + 1) * LANES]
        total = jnp.sum(product, axis=0, keepdims=True)
        squares = jnp.sum(product * product, axis=0, keepdims=True)
        found.append(mean_and_var(total, squares, rows)[1])
    var = jnp.concatenate(found, axis=1)
    block = jnp.concatenate([as_block(high), as_block(low), as_block(var)], axis=0)
    block = block.astype(jnp.bfloat16)
    message[:, : block.shape[0], :] = jnp.broadcast_to(
        block[None], (message.shape[0],) + block.shape
    )
    write_queries(message, query_feats, units)


def keys_kernel(
    columns,
    own_numbers,
    numbers,
    got,
    gain,
    shift,
    weights,
    third,
    w_key,
    frames,
    query_feats,
    w_query,
    queue,
    keys,
    message,
    pooled,
    products,
):
    clips = frames.shape[0]
    emb = queue.shape[1]
    query = jnp.dot(query_feats[...], w_query[...], preferred_element_type=jnp.float32)
    length = jnp.sqrt(jnp.sum(query * query, axis=-1, keepdims=True) + 1e-06)
    direction = query / length
    rounded = direction.astype(jnp.bfloat16)
    none, ones = jnp.zeros((clips, emb), jnp.bfloat16), jnp.ones((clips, emb), jnp.bfloat16)
    both = jnp.concatenate(
        [jnp.concatenate([rounded, none], axis=1), jnp.concatenate([none, ones], axis=1)], axis=0
    )
    step = queue.shape[0] // clips

    def queue_products(i):
        entries = queue[pl.ds(i * step, step), :]
        return lax.dot_general(
            both,
            jnp.concatenate([entries, entries * entries], axis=1),
            (((1,), (1,)), ((), ())),
            preferred_element_type=jnp.float32,
        )

    products[...] = queue_products(0)
    inner, channels = weights.shape
    part, wide = inner // LANES, channels // LANES
    same = members(numbers, group_row(own_numbers, part), part)
    picked = got[:, : 2 * part, :].astype(jnp.float32) * same
    picked = jnp.sum(picked.reshape((-1, columns) + picked.shape[1:]), axis=0)
    picked = picked[:, :part] + picked[:, part:]
    high, low = two_halves(jnp.concatenate([picked[:, j, :] for j in range(part)], axis=1))
    parts = jnp.dot(
        jnp.concatenate([high, low], axis=0).astype(jnp.bfloat16),
        weights[...],
        preferred_element_type=jnp.float32,
    )
    block_mean = parts[:columns] + parts[columns:]
    mean = jnp.sum(block_mean, axis=0, keepdims=True) / columns
    apart = block_mean - mean
    between = jnp.sum(apart * apart, axis=0, keepdims=True) / columns
    block_var = got[:, 2 * part : 2 * part + wide, :].astype(jnp.float32)
    within = as_row(jnp.sum(block_var * same, axis=0) / columns)
    scale = gain[...] * lax.rsqrt(within + between + EPSILON)
    bias = shift[...] - mean * scale

    def one_step(n, carry):
        negatives, pulled = carry
        inverse = lax.rsqrt(products[clips:] + 1e-06)
        weight = jnp.exp(products[:clips] * inverse / SHARPNESS_DIVISOR)
        negatives = negatives + jnp.sum(weight, axis=-1, keepdims=True)
        pulled = pulled + jnp.dot(
            (weight * inverse).astype(jnp.bfloat16),
            queue[pl.ds(n * step, step), :],
            preferred_element_type=jnp.float32,
        )
        products[...] = queue_products(jnp.minimum(n + 1, clips - 1))
        total = jnp.zeros((SPOTS, channels), jnp.float32)
        for t in range(FRAMES):
            values = jnp.concatenate(
                [
                    third[j, pl.ds((n * FRAMES + t) * SPOTS, SPOTS), :]
                    for j in range(wide)
                ],
                axis=1,
            )
            total = total + jnp.maximum(
                values * scale + bias + frames[n, t + 1].astype(jnp.float32), 0.0
            )
        pooled[pl.ds(n, 1), :] = jnp.sum(total, axis=0, keepdims=True) / (FRAMES * SPOTS)
        return negatives, pulled

    negatives, pulled = lax.fori_loop(
        0,
        clips,
        one_step,
        (jnp.zeros((clips, 1), jnp.float32), jnp.zeros((clips, emb), jnp.float32)),
        unroll=clips,
    )
    projected = jnp.dot(
        pooled[...].astype(jnp.bfloat16), w_key[...], preferred_element_type=jnp.float32
    )
    own = (
        projected * lax.rsqrt(jnp.sum(projected * projected, axis=-1, keepdims=True) + 1e-06)
    ).astype(jnp.bfloat16)
    keys[...] = own
    own = own.astype(jnp.float32)
    positive = jnp.exp(jnp.sum(direction * own, axis=-1, keepdims=True) / SHARPNESS_DIVISOR)
    partition = positive + negatives
    grad = (pulled / partition + (positive / partition - 1.0) * own) / SHARPNESS_DIVISOR
    radial = jnp.sum(direction * grad, axis=-1, keepdims=True)
    grad = ((grad - radial * direction) / length).astype(jnp.bfloat16)
    message[...] = jnp.broadcast_to(grad[None], message.shape)


def gradient_kernel(shares, grads, *rest):
    mine, others, (out_hbm, out, out_sem) = rest[:3], rest[3:6], rest[6:]
    devices, clips, width = grads.shape
    right = grads[...].reshape(devices * clips, width)
    half = out.shape[1]
    odd = lax.axis_index("bn") % 2

    def give(i):
        start = pl.multiple_of((odd ^ i) * half, half)
        return pltpu.make_async_copy(out.at[i], out_hbm.at[pl.ds(start, half)], out_sem.at[i])

    for i, messages in enumerate((others, mine)):
        i = 1 - i
        for units, message in zip(shares, messages):
            for j, u in enumerate(units):
                at = message.shape[1] - (len(units) - j) * clips
                queries = message[:, at : at + clips, :].reshape(devices * clips, LANES)
                out[i, u * LANES : (u + 1) * LANES] = lax.dot_general(
                    queries, right, (((0,), (0,)), ((), ())), preferred_element_type=jnp.float32
                )
        give(i).start()
    for i in range(2):
        give(i).wait()


def from_neighbour(message):
    return lax.ppermute(message, "bn", [(i, i ^ 1) for i in range(lax.axis_size("bn"))])


def exchange(message):
    return lax.all_to_all(message, ("dp", "bn"), 0, 0)


def local(
    key_feats,
    clip_starts,
    shuffle,
    query_feats,
    conv_time,
    conv_space,
    conv_expand,
    gain_one,
    shift_one,
    gain_two,
    shift_two,
    gain_three,
    shift_three,
    w_key,
    w_query,
    queue,
):
    devices = lax.axis_size("dp") * lax.axis_size("bn")
    clips, _, spots, channels = key_feats.shape
    inner, emb = conv_space.shape[1], queue.shape[1]
    part, wide = inner // LANES, channels // LANES
    rows = clips * FRAMES * spots
    count = channels // 2 // LANES
    limits = (0, 3 * count // 8, 6 * count // 8, count)
    shares = [tuple(range(a, b)) for a, b in zip(limits, limits[1:])]

    def moments_message(share):
        return jax.ShapeDtypeStruct((devices, MOMENT_ROWS + clips * len(share), LANES), jnp.bfloat16)

    row = lambda vector: vector.reshape(1, -1)

    cuts = (0, channels // 8, 3 * channels // 8, channels)
    pieces = len(cuts) - 1
    padded = (clips, FRAMES + 2, spots, channels)
    first, frames, sent_one = pl.pallas_call(
        functools.partial(time_conv_kernel, cuts, shares[0]),
        out_shape=(
            jax.ShapeDtypeStruct((part, rows + spots, LANES), jnp.float32),
            jax.ShapeDtypeStruct(padded, jnp.bfloat16),
            moments_message(shares[0]),
        ),
        in_specs=[ANY] * 5,
        out_specs=(VMEM,) * 3,
        scratch_shapes=[
            pltpu.SMEM(clip_starts.shape, jnp.int32),
            pltpu.SMEM(shuffle.shape, jnp.int32),
            pltpu.VMEM(query_feats.shape, jnp.bfloat16),
            pltpu.VMEM(conv_time.shape, jnp.bfloat16),
            pltpu.SemaphoreType.DMA((3,)),
            pltpu.SemaphoreType.DMA((pieces, clips)),
            pltpu.SemaphoreType.DMA((pieces,)),
        ],
        compiler_params=pltpu.CompilerParams(vmem_limit_bytes=20 * MIB),
        name="time_conv",
    )(
        in_hbm(clip_starts),
        in_hbm(shuffle),
        in_hbm(key_feats),
        in_hbm(conv_time),
        in_hbm(query_feats),
    )
    got_one = exchange(sent_one)
    other_one = from_neighbour(got_one)

    grid_rows = rows // spots
    pitch = grid_rows + 8
    second, sent_two = pl.pallas_call(
        functools.partial(space_conv_kernel, shares[1]),
        out_shape=(
            jax.ShapeDtypeStruct((part, SPOTS + 1, pitch, LANES), jnp.float32),
            moments_message(shares[1]),
        ),
        in_specs=[VMEM] * 7,
        out_specs=(VMEM, VMEM),
        scratch_shapes=[
            pltpu.VMEM((SIDE, SIDE, grid_rows, inner), jnp.bfloat16),
            pltpu.VMEM((SIDE, SIDE, grid_rows, inner), jnp.float32),
        ],
        compiler_params=pltpu.CompilerParams(vmem_limit_bytes=10 * MIB),
        name="space_conv",
    )(sent_one, got_one, row(gain_one), row(shift_one), first, conv_space, query_feats)
    sent_two, other_one = lax.optimization_barrier((sent_two, other_one))
    got_two = exchange(sent_two)
    other_two = from_neighbour(got_two)
    second = second.reshape(part, (SPOTS + 1) * pitch, LANES)

    third, sent = pl.pallas_call(
        functools.partial(expand_kernel, shares[2]),
        out_shape=(
            jax.ShapeDtypeStruct((wide, rows, LANES), jnp.float32),
            jax.ShapeDtypeStruct(
                (devices, 2 * part + wide + clips * len(shares[2]), LANES), jnp.bfloat16
            ),
        ),
        in_specs=[VMEM] * 7,
        out_specs=(VMEM, VMEM),
        scratch_shapes=[pltpu.VMEM((rows, inner), jnp.bfloat16)],
        compiler_params=pltpu.CompilerParams(vmem_limit_bytes=8 * MIB),
        name="expand",
    )(sent_two, got_two, row(gain_two), row(shift_two), second, conv_expand, query_feats)
    sent, other_two = lax.optimization_barrier((sent, other_two))
    got_three = exchange(sent)
    other_three = from_neighbour(got_three)

    own_keys, sent = pl.pallas_call(
        functools.partial(keys_kernel, lax.axis_size("bn")),
        out_shape=(
            jax.ShapeDtypeStruct((clips, emb), jnp.bfloat16),
            jax.ShapeDtypeStruct((devices, clips, emb), jnp.bfloat16),
        ),
        in_specs=[VMEM] * 12,
        out_specs=(VMEM, VMEM),
        scratch_shapes=[
            pltpu.VMEM((clips, channels), jnp.float32),
            pltpu.VMEM((2 * clips, queue.shape[0] // clips), jnp.float32),
        ],
        compiler_params=pltpu.CompilerParams(vmem_limit_bytes=8 * MIB),
        name="keys",
    )(
        sent_one,
        got_one,
        got_three,
        row(gain_three),
        row(shift_three),
        conv_expand,
        third,
        w_key,
        frames,
        query_feats,
        w_query,
        queue,
    )
    sent, other_three = lax.optimization_barrier((sent, other_three))
    query_grad = pl.pallas_call(
        functools.partial(gradient_kernel, shares),
        out_shape=jax.ShapeDtypeStruct((channels, emb), jnp.float32),
        in_specs=[VMEM] * 7,
        out_specs=ANY,
        scratch_shapes=[
            pltpu.VMEM((2, channels // 2, emb), jnp.float32),
            pltpu.SemaphoreType.DMA((2,)),
        ],
        compiler_params=pltpu.CompilerParams(vmem_limit_bytes=8 * MIB),
        name="query_grad",
    )(exchange(sent), got_one, got_two, got_three, other_one, other_two, other_three)
    return (own_keys, query_grad)


def solution(mesh):
    both = ("dp", "bn")
    placed = (
        P(both, None, None, None),
        P(both),
        P("bn", None),
        P(both, None),
    ) + (P(),) * 12
    return jax.shard_map(
        local, mesh=mesh, in_specs=placed, out_specs=(P(both, None), P()), check_vma=False
    )
```

```python
import functools

import jax
import jax.numpy as jnp
from jax import lax
from jax.experimental import pallas as pl
from jax.experimental.pallas import tpu as pltpu
from jax.sharding import PartitionSpec as P

FRAMES = 8
SIDE = 4
SPOTS = SIDE * SIDE
LANES = 128
SHARPNESS_DIVISOR = 0.2
EPSILON = 1e-05
MIB = 1 << 20
MOMENT_ROWS = 16

VMEM = pl.BlockSpec(memory_space=pltpu.VMEM)
ANY = pl.BlockSpec(memory_space=pl.ANY)


def in_hbm(array):
    return pltpu.with_memory_space_constraint(array, pltpu.HBM)


def as_row(block):
    return jnp.concatenate([block[i : i + 1] for i in range(block.shape[0])], axis=1)


def as_block(row):
    return jnp.concatenate(
        [row[:, i : i + LANES] for i in range(0, row.shape[1], LANES)], axis=0
    )


def write_queries(message, query_feats, units):
    half = query_feats.shape[1] // 2
    pair = jnp.stack(
        [
            jnp.concatenate(
                [
                    query_feats[:, side * half + u * LANES : side * half + (u + 1) * LANES]
                    for u in units
                ],
                axis=0,
            )
            for side in range(2)
        ]
    )
    devices, length, _ = message.shape
    every = jnp.broadcast_to(pair[None], (devices // 2,) + pair.shape)
    message[:, length - pair.shape[1] :, :] = every.reshape((devices,) + pair.shape[1:])


def two_halves(values):
    high = values.astype(jnp.bfloat16).astype(jnp.float32)
    return high, values - high


def mean_and_var(total, squares, count):
    mean = total / count
    return mean, jnp.maximum(squares / count - mean * mean, 0.0)


def write_moments(message, mean, var, group):
    high, low = two_halves(mean)
    part = [as_block(high), as_block(low), as_block(var)]
    rest = MOMENT_ROWS - sum(p.shape[0] for p in part)
    part.append(jnp.broadcast_to(group, (rest, LANES)))
    block = jnp.concatenate(part, axis=0).astype(jnp.bfloat16)
    message[:, :MOMENT_ROWS, :] = jnp.broadcast_to(block[None], (message.shape[0],) + block.shape)


def group_row(message, part):
    return message[0, 3 * part : 3 * part + 1, :].astype(jnp.float32)


def members(message, group, part):
    sender = message[:, 3 * part : 3 * part + 1, :].astype(jnp.float32)
    return (sender == group[None]).astype(jnp.float32)


def group_scale_and_bias(message, group, gain, shift):
    part = gain.shape[1] // LANES
    same = members(message, group, part)
    every = message[:, :MOMENT_ROWS, :].astype(jnp.float32)
    block_mean = every[:, :part] + every[:, part : 2 * part]
    block_var = every[:, 2 * part : 3 * part]
    blocks = jnp.sum(same, axis=0)
    mean = jnp.sum(block_mean * same, axis=0) / blocks
    apart = block_mean - mean[None]
    var = jnp.sum((block_var + apart * apart) * same, axis=0) / blocks
    scale = gain[...] * lax.rsqrt(as_row(var) + EPSILON)
    return scale, shift[...] - as_row(mean) * scale


def time_conv_kernel(
    cuts,
    units,
    starts_hbm,
    shuffle_hbm,
    feats,
    weights,
    queries_hbm,
    first,
    frames,
    message,
    starts,
    shuffle,
    query_feats,
    taps,
    small_sem,
    frames_sem,
    taps_sem,
):
    clips, _, spots, _ = feats.shape
    inner = weights.shape[2]
    pieces = len(cuts) - 1
    rows = clips * FRAMES * spots
    span = [pl.ds(cuts[k], cuts[k + 1] - cuts[k]) for k in range(pieces)]

    def copy_clip(k, n):
        return pltpu.make_async_copy(
            feats.at[n, pl.ds(starts[n], FRAMES), :, span[k]],
            frames.at[n, pl.ds(1, FRAMES), :, span[k]],
            frames_sem.at[k, n],
        )

    def copy_taps(k):
        return pltpu.make_async_copy(
            weights.at[:, span[k], :], taps.at[:, span[k], :], taps_sem.at[k]
        )

    copy_starts = pltpu.make_async_copy(starts_hbm, starts, small_sem.at[0])
    copy_shuffle = pltpu.make_async_copy(shuffle_hbm, shuffle, small_sem.at[1])
    copy_queries = pltpu.make_async_copy(queries_hbm, query_feats, small_sem.at[2])
    copy_starts.start()
    copy_shuffle.start()
    copy_taps(0).start()
    copy_starts.wait()
    for k in range(pieces):
        for n in range(clips):
            copy_clip(k, n).start()
        if k + 1 < pieces:
            copy_taps(k + 1).start()
    copy_queries.start()
    blank = jnp.zeros((clips, 1) + frames.shape[2:], jnp.bfloat16)
    frames[:, 0:1] = blank
    frames[:, FRAMES + 1 : FRAMES + 2] = blank
    total, squares = [], []
    for k in range(pieces):
        depth = cuts[k + 1] - cuts[k]
        copy_taps(k).wait()
        for n in range(clips):
            copy_clip(k, n).wait()
        stacked = jnp.concatenate(
            [
                frames[:, o : o + FRAMES, :, cuts[k] : cuts[k + 1]].reshape(rows, depth)
                for o in range(3)
            ],
            axis=1,
        )
        product = jnp.dot(
            stacked,
            taps[:, cuts[k] : cuts[k + 1], :].reshape(3 * depth, inner),
            preferred_element_type=jnp.float32,
        )
        for j in range(inner // LANES):
            piece = product[:, j * LANES : (j + 1) * LANES]
            if k > 0:
                piece = piece + first[j, :rows]
            first[j, :rows] = piece
            if k == pieces - 1:
                total.append(jnp.sum(piece, axis=0, keepdims=True))
                squares.append(jnp.sum(piece * piece, axis=0, keepdims=True))
    mean, var = mean_and_var(
        jnp.concatenate(total, axis=1), jnp.concatenate(squares, axis=1), rows
    )
    copy_shuffle.wait()
    group = shuffle[0, lax.axis_index("dp")].astype(jnp.float32)
    write_moments(message, mean, var, jnp.full((1, LANES), group, jnp.float32))
    copy_queries.wait()
    write_queries(message, query_feats, units)


def space_conv_kernel(
    units, own, got, gain, shift, first, weights, query_feats, second, message, act, taken
):
    inner = weights.shape[1]
    part = inner // LANES
    rows = act.shape[2]
    number = group_row(own, part)
    scale, bias = group_scale_and_bias(got, number, gain, shift)
    for r in range(SIDE):
        for c in range(SIDE):
            values = jnp.concatenate(
                [first[j, pl.ds(r * SIDE + c, rows, stride=SPOTS), :] for j in range(part)],
                axis=1,
            )
            act[r, c] = jnp.maximum(values * scale + bias, 0.0).astype(jnp.bfloat16)
    for k in (4, 0, 1, 2, 3, 5, 6, 7, 8):
        down, right = k // 3 - 1, k % 3 - 1
        r0, r1 = max(0, -down), min(SIDE, SIDE - down)
        c0, c1 = max(0, -right), min(SIDE, SIDE - right)
        source = act[r0 + down : r1 + down, c0 + right : c1 + right]
        product = jnp.dot(
            source.reshape((r1 - r0) * (c1 - c0) * rows, inner),
            weights[k],
            preferred_element_type=jnp.float32,
        ).reshape(r1 - r0, c1 - c0, rows, inner)
        if k == 4:
            taken[...] = product
        else:
            taken[r0:r1, c0:c1] += product
    total = jnp.zeros((1, inner), jnp.float32)
    squares = jnp.zeros((1, inner), jnp.float32)
    for r in range(SIDE):
        for c in range(SIDE):
            values = taken[r, c]
            for j in range(part):
                second[j, r * SIDE + c, 0:rows] = values[:, j * LANES : (j + 1) * LANES]
            total = total + jnp.sum(values, axis=0, keepdims=True)
            squares = squares + jnp.sum(values * values, axis=0, keepdims=True)
    mean, var = mean_and_var(total, squares, rows * SPOTS)
    write_moments(message, mean, var, number)
    write_queries(message, query_feats, units)


def expand_kernel(
    units, own, got, gain, shift, second, weights, query_feats, third, message, act):
    inner, channels = weights.shape
    rows = act.shape[0]
    part = inner // LANES
    scale, bias = group_scale_and_bias(got, group_row(own, part), gain, shift)
    pitch = second.shape[1] // (SPOTS + 1)
    total = jnp.zeros((SPOTS, inner), jnp.float32)
    for i in range(rows // SPOTS):
        values = jnp.concatenate(
            [second[j, pl.ds(i, SPOTS, stride=pitch), :] for j in range(part)], axis=1
        )
        act_two = jnp.maximum(values * scale + bias, 0.0).astype(jnp.bfloat16)
        act[i * SPOTS : (i + 1) * SPOTS] = act_two
        total = total + act_two.astype(jnp.float32)
    act_mean = jnp.sum(total, axis=0, keepdims=True) / rows
    high, low = two_halves(act_mean)
    found = []
    width = 4 * LANES
    for start in range(0, channels, width):
        product = jnp.dot(
            act[...], weights[:, start : start + width], preferred_element_type=jnp.float32
        )
        for j in range(width // LANES):
            third[start // LANES + j] = product[:, j * LANES : (j + 1) * LANES]
        total = jnp.sum(product, axis=0, keepdims=True)
        squares = jnp.sum(product * product, axis=0, keepdims=True)
        found.append(mean_and_var(total, squares, rows)[1])
    var = jnp.concatenate(found, axis=1)
    block = jnp.concatenate([as_block(high), as_block(low), as_block(var)], axis=0)
    block = block.astype(jnp.bfloat16)
    message[:, : block.shape[0], :] = jnp.broadcast_to(
        block[None], (message.shape[0],) + block.shape
    )
    write_queries(message, query_feats, units)


def keys_kernel(
    columns,
    own_numbers,
    numbers,
    got,
    gain,
    shift,
    weights,
    third,
    w_key,
    frames,
    query_feats,
    w_query,
    queue,
    keys,
    message,
    pooled,
    products,
):
    clips = frames.shape[0]
    emb = queue.shape[1]
    query = jnp.dot(query_feats[...], w_query[...], preferred_element_type=jnp.float32)
    length = jnp.sqrt(jnp.sum(query * query, axis=-1, keepdims=True) + 1e-06)
    direction = query / length
    rounded = direction.astype(jnp.bfloat16)
    none, ones = jnp.zeros((clips, emb), jnp.bfloat16), jnp.ones((clips, emb), jnp.bfloat16)
    both = jnp.concatenate(
        [jnp.concatenate([rounded, none], axis=1), jnp.concatenate([none, ones], axis=1)], axis=0
    )
    step = queue.shape[0] // clips

    def queue_products(i):
        entries = queue[i * step : (i + 1) * step, :]
        return lax.dot_general(
            both,
            jnp.concatenate([entries, entries * entries], axis=1),
            (((1,), (1,)), ((), ())),
            preferred_element_type=jnp.float32,
        )

    products[...] = queue_products(0)
    inner, channels = weights.shape
    part, wide = inner // LANES, channels // LANES
    same = members(numbers, group_row(own_numbers, part), part)
    picked = got[:, : 2 * part, :].astype(jnp.float32) * same
    picked = jnp.sum(picked.reshape((-1, columns) + picked.shape[1:]), axis=0)
    picked = picked[:, :part] + picked[:, part:]
    high, low = two_halves(jnp.concatenate([picked[:, j, :] for j in range(part)], axis=1))
    parts = jnp.dot(
        jnp.concatenate([high, low], axis=0).astype(jnp.bfloat16),
        weights[...],
        preferred_element_type=jnp.float32,
    )
    block_mean = parts[:columns] + parts[columns:]
    mean = jnp.sum(block_mean, axis=0, keepdims=True) / columns
    apart = block_mean - mean
    between = jnp.sum(apart * apart, axis=0, keepdims=True) / columns
    block_var = got[:, 2 * part : 2 * part + wide, :].astype(jnp.float32)
    within = as_row(jnp.sum(block_var * same, axis=0) / columns)
    scale = gain[...] * lax.rsqrt(within + between + EPSILON)
    bias = shift[...] - mean * scale

    negatives = jnp.zeros((clips, 1), jnp.float32)
    pulled = jnp.zeros((clips, emb), jnp.float32)
    length_of_clip = FRAMES * SPOTS
    for n in range(clips):
        current = products[...]
        if n + 1 < clips:
            products[...] = queue_products(n + 1)
        inverse = lax.rsqrt(current[clips:] + 1e-06)
        weight = jnp.exp(current[:clips] * inverse / SHARPNESS_DIVISOR)
        negatives = negatives + jnp.sum(weight, axis=-1, keepdims=True)
        pulled = pulled + jnp.dot(
            (weight * inverse).astype(jnp.bfloat16),
            queue[n * step : (n + 1) * step, :],
            preferred_element_type=jnp.float32,
        )
        for j in range(wide):
            lanes = slice(j * LANES, (j + 1) * LANES)
            chosen = frames[n, 1 : FRAMES + 1, :, lanes].reshape(length_of_clip, LANES)
            merged = jnp.maximum(
                third[j, n * length_of_clip : (n + 1) * length_of_clip, :] * scale[:, lanes]
                + bias[:, lanes]
                + chosen.astype(jnp.float32),
                0.0,
            )
            pooled[n : n + 1, lanes] = (
                jnp.sum(merged, axis=0, keepdims=True) / length_of_clip
            )
    projected = jnp.dot(
        pooled[...].astype(jnp.bfloat16), w_key[...], preferred_element_type=jnp.float32
    )
    own = (
        projected * lax.rsqrt(jnp.sum(projected * projected, axis=-1, keepdims=True) + 1e-06)
    ).astype(jnp.bfloat16)
    keys[...] = own
    own = own.astype(jnp.float32)
    positive = jnp.exp(jnp.sum(direction * own, axis=-1, keepdims=True) / SHARPNESS_DIVISOR)
    partition = positive + negatives
    grad = (pulled / partition + (positive / partition - 1.0) * own) / SHARPNESS_DIVISOR
    radial = jnp.sum(direction * grad, axis=-1, keepdims=True)
    grad = ((grad - radial * direction) / length).astype(jnp.bfloat16)
    message[...] = jnp.broadcast_to(grad[None], message.shape)


def gradient_kernel(shares, grads, *rest):
    mine, others, (out_hbm, out, out_sem) = rest[:3], rest[3:6], rest[6:]
    devices, clips, width = grads.shape
    right = grads[...].reshape(devices * clips, width)
    half = out.shape[1]
    odd = lax.axis_index("bn") % 2

    def give(i):
        start = pl.multiple_of((odd ^ i) * half, half)
        return pltpu.make_async_copy(out.at[i], out_hbm.at[pl.ds(start, half)], out_sem.at[i])

    for i, messages in enumerate((others, mine)):
        i = 1 - i
        for units, message in zip(shares, messages):
            for j, u in enumerate(units):
                at = message.shape[1] - (len(units) - j) * clips
                queries = message[:, at : at + clips, :].reshape(devices * clips, LANES)
                out[i, u * LANES : (u + 1) * LANES] = lax.dot_general(
                    queries, right, (((0,), (0,)), ((), ())), preferred_element_type=jnp.float32
                )
        give(i).start()
    for i in range(2):
        give(i).wait()


def from_neighbour(message):
    return lax.ppermute(message, "bn", [(i, i ^ 1) for i in range(lax.axis_size("bn"))])


def exchange(message):
    return lax.all_to_all(message, ("dp", "bn"), 0, 0)


def local(
    key_feats,
    clip_starts,
    shuffle,
    query_feats,
    conv_time,
    conv_space,
    conv_expand,
    gain_one,
    shift_one,
    gain_two,
    shift_two,
    gain_three,
    shift_three,
    w_key,
    w_query,
    queue,
):
    devices = lax.axis_size("dp") * lax.axis_size("bn")
    clips, _, spots, channels = key_feats.shape
    inner, emb = conv_space.shape[1], queue.shape[1]
    part, wide = inner // LANES, channels // LANES
    rows = clips * FRAMES * spots
    count = channels // 2 // LANES
    limits = (0, 3 * count // 8, 6 * count // 8, count)
    shares = [tuple(range(a, b)) for a, b in zip(limits, limits[1:])]

    def moments_message(share):
        return jax.ShapeDtypeStruct((devices, MOMENT_ROWS + clips * len(share), LANES), jnp.bfloat16)

    row = lambda vector: vector.reshape(1, -1)

    cuts = (0, channels // 8, 3 * channels // 8, channels)
    pieces = len(cuts) - 1
    padded = (clips, FRAMES + 2, spots, channels)
    first, frames, sent_one = pl.pallas_call(
        functools.partial(time_conv_kernel, cuts, shares[0]),
        out_shape=(
            jax.ShapeDtypeStruct((part, rows + spots, LANES), jnp.float32),
            jax.ShapeDtypeStruct(padded, jnp.bfloat16),
            moments_message(shares[0]),
        ),
        in_specs=[ANY] * 5,
        out_specs=(VMEM,) * 3,
        scratch_shapes=[
            pltpu.SMEM(clip_starts.shape, jnp.int32),
            pltpu.SMEM(shuffle.shape, jnp.int32),
            pltpu.VMEM(query_feats.shape, jnp.bfloat16),
            pltpu.VMEM(conv_time.shape, jnp.bfloat16),
            pltpu.SemaphoreType.DMA((3,)),
            pltpu.SemaphoreType.DMA((pieces, clips)),
            pltpu.SemaphoreType.DMA((pieces,)),
        ],
        compiler_params=pltpu.CompilerParams(vmem_limit_bytes=20 * MIB),
        name="time_conv",
    )(
        in_hbm(clip_starts),
        in_hbm(shuffle),
        in_hbm(key_feats),
        in_hbm(conv_time),
        in_hbm(query_feats),
    )
    got_one = exchange(sent_one)
    other_one = from_neighbour(got_one)

    grid_rows = rows // spots
    pitch = grid_rows + 8
    second, sent_two = pl.pallas_call(
        functools.partial(space_conv_kernel, shares[1]),
        out_shape=(
            jax.ShapeDtypeStruct((part, SPOTS + 1, pitch, LANES), jnp.float32),
            moments_message(shares[1]),
        ),
        in_specs=[VMEM] * 7,
        out_specs=(VMEM, VMEM),
        scratch_shapes=[
            pltpu.VMEM((SIDE, SIDE, grid_rows, inner), jnp.bfloat16),
            pltpu.VMEM((SIDE, SIDE, grid_rows, inner), jnp.float32),
        ],
        compiler_params=pltpu.CompilerParams(vmem_limit_bytes=10 * MIB),
        name="space_conv",
    )(sent_one, got_one, row(gain_one), row(shift_one), first, conv_space, query_feats)
    sent_two, other_one = lax.optimization_barrier((sent_two, other_one))
    got_two = exchange(sent_two)
    other_two = from_neighbour(got_two)
    second = second.reshape(part, (SPOTS + 1) * pitch, LANES)

    third, sent = pl.pallas_call(
        functools.partial(expand_kernel, shares[2]),
        out_shape=(
            jax.ShapeDtypeStruct((wide, rows, LANES), jnp.float32),
            jax.ShapeDtypeStruct(
                (devices, 2 * part + wide + clips * len(shares[2]), LANES), jnp.bfloat16
            ),
        ),
        in_specs=[VMEM] * 7,
        out_specs=(VMEM, VMEM),
        scratch_shapes=[pltpu.VMEM((rows, inner), jnp.bfloat16)],
        compiler_params=pltpu.CompilerParams(vmem_limit_bytes=8 * MIB),
        name="expand",
    )(sent_two, got_two, row(gain_two), row(shift_two), second, conv_expand, query_feats)
    sent, other_two = lax.optimization_barrier((sent, other_two))
    got_three = exchange(sent)
    other_three = from_neighbour(got_three)

    own_keys, sent = pl.pallas_call(
        functools.partial(keys_kernel, lax.axis_size("bn")),
        out_shape=(
            jax.ShapeDtypeStruct((clips, emb), jnp.bfloat16),
            jax.ShapeDtypeStruct((devices, clips, emb), jnp.bfloat16),
        ),
        in_specs=[VMEM] * 12,
        out_specs=(VMEM, VMEM),
        scratch_shapes=[
            pltpu.VMEM((clips, channels), jnp.float32),
            pltpu.VMEM((2 * clips, queue.shape[0] // clips), jnp.float32),
        ],
        compiler_params=pltpu.CompilerParams(vmem_limit_bytes=8 * MIB),
        name="keys",
    )(
        sent_one,
        got_one,
        got_three,
        row(gain_three),
        row(shift_three),
        conv_expand,
        third,
        w_key,
        frames,
        query_feats,
        w_query,
        queue,
    )
    sent, other_three = lax.optimization_barrier((sent, other_three))
    query_grad = pl.pallas_call(
        functools.partial(gradient_kernel, shares),
        out_shape=jax.ShapeDtypeStruct((channels, emb), jnp.float32),
        in_specs=[VMEM] * 7,
        out_specs=ANY,
        scratch_shapes=[
            pltpu.VMEM((2, channels // 2, emb), jnp.float32),
            pltpu.SemaphoreType.DMA((2,)),
        ],
        compiler_params=pltpu.CompilerParams(vmem_limit_bytes=8 * MIB),
        name="query_grad",
    )(exchange(sent), got_one, got_two, got_three, other_one, other_two, other_three)
    return (own_keys, query_grad)


def solution(mesh):
    both = ("dp", "bn")
    placed = (
        P(both, None, None, None),
        P(both),
        P("bn", None),
        P(both, None),
    ) + (P(),) * 12
    return jax.shard_map(
        local, mesh=mesh, in_specs=placed, out_specs=(P(both, None), P()), check_vma=False
    )
```

```python
import functools

import jax
import jax.numpy as jnp
from jax import lax
from jax.experimental import pallas as pl
from jax.experimental.pallas import tpu as pltpu
from jax.sharding import PartitionSpec as P

FRAMES = 8
SIDE = 4
SPOTS = SIDE * SIDE
LANES = 128
SHARPNESS_DIVISOR = 0.2
EPSILON = 1e-05
MIB = 1 << 20
MOMENT_ROWS = 16

VMEM = pl.BlockSpec(memory_space=pltpu.VMEM)
ANY = pl.BlockSpec(memory_space=pl.ANY)


def in_hbm(array):
    return pltpu.with_memory_space_constraint(array, pltpu.HBM)


def as_row(block):
    return jnp.concatenate([block[i : i + 1] for i in range(block.shape[0])], axis=1)


def as_block(row):
    return jnp.concatenate(
        [row[:, i : i + LANES] for i in range(0, row.shape[1], LANES)], axis=0
    )


def write_queries(message, query_feats, units):
    half = query_feats.shape[1] // 2
    pair = jnp.stack(
        [
            jnp.concatenate(
                [
                    query_feats[:, side * half + u * LANES : side * half + (u + 1) * LANES]
                    for u in units
                ],
                axis=0,
            )
            for side in range(2)
        ]
    )
    devices, length, _ = message.shape
    every = jnp.broadcast_to(pair[None], (devices // 2,) + pair.shape)
    message[:, length - pair.shape[1] :, :] = every.reshape((devices,) + pair.shape[1:])


def two_halves(values):
    high = values.astype(jnp.bfloat16).astype(jnp.float32)
    return high, values - high


def mean_and_var(total, squares, count):
    mean = total / count
    return mean, jnp.maximum(squares / count - mean * mean, 0.0)


def write_moments(message, mean, var, group):
    high, low = two_halves(mean)
    part = [as_block(high), as_block(low), as_block(var)]
    rest = MOMENT_ROWS - sum(p.shape[0] for p in part)
    part.append(jnp.broadcast_to(group, (rest, LANES)))
    block = jnp.concatenate(part, axis=0).astype(jnp.bfloat16)
    message[:, :MOMENT_ROWS, :] = jnp.broadcast_to(block[None], (message.shape[0],) + block.shape)


def group_row(message, part):
    return message[0, 3 * part : 3 * part + 1, :].astype(jnp.float32)


def members(message, group, part):
    sender = message[:, 3 * part : 3 * part + 1, :].astype(jnp.float32)
    return (sender == group[None]).astype(jnp.float32)


def group_scale_and_bias(message, group, gain, shift):
    part = gain.shape[1] // LANES
    same = members(message, group, part)
    every = message[:, :MOMENT_ROWS, :].astype(jnp.float32)
    block_mean = every[:, :part] + every[:, part : 2 * part]
    block_var = every[:, 2 * part : 3 * part]
    blocks = jnp.sum(same, axis=0)
    mean = jnp.sum(block_mean * same, axis=0) / blocks
    apart = block_mean - mean[None]
    var = jnp.sum((block_var + apart * apart) * same, axis=0) / blocks
    scale = gain[...] * lax.rsqrt(as_row(var) + EPSILON)
    return scale, shift[...] - as_row(mean) * scale


def time_conv_kernel(
    cuts,
    units,
    starts_hbm,
    shuffle_hbm,
    feats,
    weights,
    queries_hbm,
    first,
    frames,
    message,
    starts,
    shuffle,
    query_feats,
    taps,
    small_sem,
    frames_sem,
    taps_sem,
):
    clips, _, spots, _ = feats.shape
    inner = weights.shape[2]
    pieces = len(cuts) - 1
    rows = clips * FRAMES * spots
    span = [pl.ds(cuts[k], cuts[k + 1] - cuts[k]) for k in range(pieces)]

    def copy_clip(k, n):
        return pltpu.make_async_copy(
            feats.at[n, pl.ds(starts[n], FRAMES), :, span[k]],
            frames.at[n, pl.ds(1, FRAMES), :, span[k]],
            frames_sem.at[k, n],
        )

    def copy_taps(k):
        return pltpu.make_async_copy(
            weights.at[:, span[k], :], taps.at[:, span[k], :], taps_sem.at[k]
        )

    copy_starts = pltpu.make_async_copy(starts_hbm, starts, small_sem.at[0])
    copy_shuffle = pltpu.make_async_copy(shuffle_hbm, shuffle, small_sem.at[1])
    copy_queries = pltpu.make_async_copy(queries_hbm, query_feats, small_sem.at[2])
    copy_starts.start()
    copy_shuffle.start()
    copy_taps(0).start()
    copy_starts.wait()
    for k in range(pieces):
        for n in range(clips):
            copy_clip(k, n).start()
        if k + 1 < pieces:
            copy_taps(k + 1).start()
    copy_queries.start()
    blank = jnp.zeros((clips, 1) + frames.shape[2:], jnp.bfloat16)
    frames[:, 0:1] = blank
    frames[:, FRAMES + 1 : FRAMES + 2] = blank
    total, squares = [], []
    for k in range(pieces):
        depth = cuts[k + 1] - cuts[k]
        copy_taps(k).wait()
        for n in range(clips):
            copy_clip(k, n).wait()
        stacked = jnp.concatenate(
            [
                frames[:, o : o + FRAMES, :, cuts[k] : cuts[k + 1]].reshape(rows, depth)
                for o in range(3)
            ],
            axis=1,
        )
        product = jnp.dot(
            stacked,
            taps[:, cuts[k] : cuts[k + 1], :].reshape(3 * depth, inner),
            preferred_element_type=jnp.float32,
        )
        for j in range(inner // LANES):
            piece = product[:, j * LANES : (j + 1) * LANES]
            if k > 0:
                piece = piece + first[j, :rows]
            first[j, :rows] = piece
            if k == pieces - 1:
                total.append(jnp.sum(piece, axis=0, keepdims=True))
                squares.append(jnp.sum(piece * piece, axis=0, keepdims=True))
    mean, var = mean_and_var(
        jnp.concatenate(total, axis=1), jnp.concatenate(squares, axis=1), rows
    )
    copy_shuffle.wait()
    group = shuffle[0, lax.axis_index("dp")].astype(jnp.float32)
    write_moments(message, mean, var, jnp.full((1, LANES), group, jnp.float32))
    copy_queries.wait()
    write_queries(message, query_feats, units)


def space_conv_kernel(
    units, own, got, gain, shift, first, weights, query_feats, second, message, act, taken
):
    inner = weights.shape[1]
    part = inner // LANES
    rows = act.shape[2]
    number = group_row(own, part)
    scale, bias = group_scale_and_bias(got, number, gain, shift)
    for r in range(SIDE):
        for c in range(SIDE):
            values = jnp.concatenate(
                [first[j, pl.ds(r * SIDE + c, rows, stride=SPOTS), :] for j in range(part)],
                axis=1,
            )
            act[r, c] = jnp.maximum(values * scale + bias, 0.0).astype(jnp.bfloat16)
    taken[0:1] = jnp.zeros((1,) + taken.shape[1:], jnp.float32)
    for k in (1, 0, 2, 3, 5, 6, 7, 8, 4):
        down, right = k // 3 - 1, k % 3 - 1
        r0, r1 = max(0, -down), min(SIDE, SIDE - down)
        c0, c1 = max(0, -right), min(SIDE, SIDE - right)
        source = act[r0 + down : r1 + down, c0 + right : c1 + right]
        product = jnp.dot(
            source.reshape((r1 - r0) * (c1 - c0) * rows, inner),
            weights[k],
            preferred_element_type=jnp.float32,
        ).reshape(r1 - r0, c1 - c0, rows, inner)
        if k == 1:
            taken[r0:r1, c0:c1] = product
        elif k != 4:
            taken[r0:r1, c0:c1] += product
    total = jnp.zeros((1, inner), jnp.float32)
    squares = jnp.zeros((1, inner), jnp.float32)
    for r in range(SIDE):
        for c in range(SIDE):
            values = taken[r, c] + product[r, c]
            for j in range(part):
                second[j, r * SIDE + c, 0:rows] = values[:, j * LANES : (j + 1) * LANES]
            total = total + jnp.sum(values, axis=0, keepdims=True)
            squares = squares + jnp.sum(values * values, axis=0, keepdims=True)
    mean, var = mean_and_var(total, squares, rows * SPOTS)
    write_moments(message, mean, var, number)
    write_queries(message, query_feats, units)


def expand_kernel(
    units, own, got, gain, shift, second, weights, query_feats, third, message, act):
    inner, channels = weights.shape
    rows = act.shape[0]
    part = inner // LANES
    scale, bias = group_scale_and_bias(got, group_row(own, part), gain, shift)
    pitch = second.shape[1] // (SPOTS + 1)
    total = jnp.zeros((SPOTS, inner), jnp.float32)
    for i in range(rows // SPOTS):
        values = jnp.concatenate(
            [second[j, pl.ds(i, SPOTS, stride=pitch), :] for j in range(part)], axis=1
        )
        act_two = jnp.maximum(values * scale + bias, 0.0).astype(jnp.bfloat16)
        act[i * SPOTS : (i + 1) * SPOTS] = act_two
        total = total + act_two.astype(jnp.float32)
    act_mean = jnp.sum(total, axis=0, keepdims=True) / rows
    high, low = two_halves(act_mean)
    found = []
    width = 4 * LANES
    for start in range(0, channels, width):
        product = jnp.dot(
            act[...], weights[:, start : start + width], preferred_element_type=jnp.float32
        )
        for j in range(width // LANES):
            third[start // LANES + j] = product[:, j * LANES : (j + 1) * LANES]
        total = jnp.sum(product, axis=0, keepdims=True)
        squares = jnp.sum(product * product, axis=0, keepdims=True)
        found.append(mean_and_var(total, squares, rows)[1])
    var = jnp.concatenate(found, axis=1)
    block = jnp.concatenate([as_block(high), as_block(low), as_block(var)], axis=0)
    block = block.astype(jnp.bfloat16)
    message[:, : block.shape[0], :] = jnp.broadcast_to(
        block[None], (message.shape[0],) + block.shape
    )
    write_queries(message, query_feats, units)


def keys_kernel(
    columns,
    own_numbers,
    numbers,
    got,
    gain,
    shift,
    weights,
    third,
    w_key,
    frames,
    query_feats,
    w_query,
    queue,
    keys,
    message,
    pooled,
    products,
):
    clips = frames.shape[0]
    emb = queue.shape[1]
    query = jnp.dot(query_feats[...], w_query[...], preferred_element_type=jnp.float32)
    length = jnp.sqrt(jnp.sum(query * query, axis=-1, keepdims=True) + 1e-06)
    direction = query / length
    rounded = direction.astype(jnp.bfloat16)
    none, ones = jnp.zeros((clips, emb), jnp.bfloat16), jnp.ones((clips, emb), jnp.bfloat16)
    both = jnp.concatenate(
        [jnp.concatenate([rounded, none], axis=1), jnp.concatenate([none, ones], axis=1)], axis=0
    )
    step = queue.shape[0] // clips

    def queue_products(i):
        entries = queue[i * step : (i + 1) * step, :]
        return lax.dot_general(
            both,
            jnp.concatenate([entries, entries * entries], axis=1),
            (((1,), (1,)), ((), ())),
            preferred_element_type=jnp.float32,
        )

    products[...] = queue_products(0)
    inner, channels = weights.shape
    part, wide = inner // LANES, channels // LANES
    same = members(numbers, group_row(own_numbers, part), part)
    picked = got[:, : 2 * part, :].astype(jnp.float32) * same
    picked = jnp.sum(picked.reshape((-1, columns) + picked.shape[1:]), axis=0)
    picked = picked[:, :part] + picked[:, part:]
    high, low = two_halves(jnp.concatenate([picked[:, j, :] for j in range(part)], axis=1))
    parts = jnp.dot(
        jnp.concatenate([high, low], axis=0).astype(jnp.bfloat16),
        weights[...],
        preferred_element_type=jnp.float32,
    )
    block_mean = parts[:columns] + parts[columns:]
    mean = jnp.sum(block_mean, axis=0, keepdims=True) / columns
    apart = block_mean - mean
    between = jnp.sum(apart * apart, axis=0, keepdims=True) / columns
    block_var = got[:, 2 * part : 2 * part + wide, :].astype(jnp.float32)
    within = as_row(jnp.sum(block_var * same, axis=0) / columns)
    scale = gain[...] * lax.rsqrt(within + between + EPSILON)
    bias = shift[...] - mean * scale

    negatives = jnp.zeros((clips, 1), jnp.float32)
    pulled = jnp.zeros((clips, emb), jnp.float32)
    length_of_clip = FRAMES * SPOTS
    for n in range(clips):
        current = products[...]
        if n + 1 < clips:
            products[...] = queue_products(n + 1)
        inverse = lax.rsqrt(current[clips:] + 1e-06)
        weight = jnp.exp(current[:clips] * inverse / SHARPNESS_DIVISOR)
        negatives = negatives + jnp.sum(weight, axis=-1, keepdims=True)
        pulled = pulled + jnp.dot(
            (weight * inverse).astype(jnp.bfloat16),
            queue[n * step : (n + 1) * step, :],
            preferred_element_type=jnp.float32,
        )
        for j in range(wide):
            lanes = slice(j * LANES, (j + 1) * LANES)
            chosen = frames[n, 1 : FRAMES + 1, :, lanes].reshape(length_of_clip, LANES)
            merged = jnp.maximum(
                third[j, n * length_of_clip : (n + 1) * length_of_clip, :] * scale[:, lanes]
                + bias[:, lanes]
                + chosen.astype(jnp.float32),
                0.0,
            )
            pooled[n : n + 1, lanes] = (
                jnp.sum(merged, axis=0, keepdims=True) / length_of_clip
            )
    projected = jnp.dot(
        pooled[...].astype(jnp.bfloat16), w_key[...], preferred_element_type=jnp.float32
    )
    own = (
        projected * lax.rsqrt(jnp.sum(projected * projected, axis=-1, keepdims=True) + 1e-06)
    ).astype(jnp.bfloat16)
    keys[...] = own
    own = own.astype(jnp.float32)
    positive = jnp.exp(jnp.sum(direction * own, axis=-1, keepdims=True) / SHARPNESS_DIVISOR)
    partition = positive + negatives
    grad = (pulled / partition + (positive / partition - 1.0) * own) / SHARPNESS_DIVISOR
    radial = jnp.sum(direction * grad, axis=-1, keepdims=True)
    grad = ((grad - radial * direction) / length).astype(jnp.bfloat16)
    message[...] = jnp.broadcast_to(grad[None], message.shape)


def gradient_kernel(shares, grads, *rest):
    mine, others, (out_hbm, out, out_sem) = rest[:3], rest[3:6], rest[6:]
    devices, clips, width = grads.shape
    right = grads[...].reshape(devices * clips, width)
    half = out.shape[1]
    odd = lax.axis_index("bn") % 2

    def give(i):
        start = pl.multiple_of((odd ^ i) * half, half)
        return pltpu.make_async_copy(out.at[i], out_hbm.at[pl.ds(start, half)], out_sem.at[i])

    for i, messages in enumerate((others, mine)):
        i = 1 - i
        for units, message in zip(shares, messages):
            for j, u in enumerate(units):
                at = message.shape[1] - (len(units) - j) * clips
                queries = message[:, at : at + clips, :].reshape(devices * clips, LANES)
                out[i, u * LANES : (u + 1) * LANES] = lax.dot_general(
                    queries, right, (((0,), (0,)), ((), ())), preferred_element_type=jnp.float32
                )
        give(i).start()
    for i in range(2):
        give(i).wait()


def from_neighbour(message):
    return lax.ppermute(message, "bn", [(i, i ^ 1) for i in range(lax.axis_size("bn"))])


def exchange(message):
    return lax.all_to_all(message, ("dp", "bn"), 0, 0)


def local(
    key_feats,
    clip_starts,
    shuffle,
    query_feats,
    conv_time,
    conv_space,
    conv_expand,
    gain_one,
    shift_one,
    gain_two,
    shift_two,
    gain_three,
    shift_three,
    w_key,
    w_query,
    queue,
):
    devices = lax.axis_size("dp") * lax.axis_size("bn")
    clips, _, spots, channels = key_feats.shape
    inner, emb = conv_space.shape[1], queue.shape[1]
    part, wide = inner // LANES, channels // LANES
    rows = clips * FRAMES * spots
    count = channels // 2 // LANES
    limits = (0, 3 * count // 8, 6 * count // 8, count)
    shares = [tuple(range(a, b)) for a, b in zip(limits, limits[1:])]

    def moments_message(share):
        return jax.ShapeDtypeStruct((devices, MOMENT_ROWS + clips * len(share), LANES), jnp.bfloat16)

    row = lambda vector: vector.reshape(1, -1)

    cuts = (0, channels // 8, 3 * channels // 8, channels)
    pieces = len(cuts) - 1
    padded = (clips, FRAMES + 2, spots, channels)
    first, frames, sent_one = pl.pallas_call(
        functools.partial(time_conv_kernel, cuts, shares[0]),
        out_shape=(
            jax.ShapeDtypeStruct((part, rows + spots, LANES), jnp.float32),
            jax.ShapeDtypeStruct(padded, jnp.bfloat16),
            moments_message(shares[0]),
        ),
        in_specs=[ANY] * 5,
        out_specs=(VMEM,) * 3,
        scratch_shapes=[
            pltpu.SMEM(clip_starts.shape, jnp.int32),
            pltpu.SMEM(shuffle.shape, jnp.int32),
            pltpu.VMEM(query_feats.shape, jnp.bfloat16),
            pltpu.VMEM(conv_time.shape, jnp.bfloat16),
            pltpu.SemaphoreType.DMA((3,)),
            pltpu.SemaphoreType.DMA((pieces, clips)),
            pltpu.SemaphoreType.DMA((pieces,)),
        ],
        compiler_params=pltpu.CompilerParams(vmem_limit_bytes=20 * MIB),
        name="time_conv",
    )(
        in_hbm(clip_starts),
        in_hbm(shuffle),
        in_hbm(key_feats),
        in_hbm(conv_time),
        in_hbm(query_feats),
    )
    got_one = exchange(sent_one)
    other_one = from_neighbour(got_one)

    grid_rows = rows // spots
    pitch = grid_rows + 8
    second, sent_two = pl.pallas_call(
        functools.partial(space_conv_kernel, shares[1]),
        out_shape=(
            jax.ShapeDtypeStruct((part, SPOTS + 1, pitch, LANES), jnp.float32),
            moments_message(shares[1]),
        ),
        in_specs=[VMEM] * 7,
        out_specs=(VMEM, VMEM),
        scratch_shapes=[
            pltpu.VMEM((SIDE, SIDE, grid_rows, inner), jnp.bfloat16),
            pltpu.VMEM((SIDE, SIDE, grid_rows, inner), jnp.float32),
        ],
        compiler_params=pltpu.CompilerParams(vmem_limit_bytes=10 * MIB),
        name="space_conv",
    )(sent_one, got_one, row(gain_one), row(shift_one), first, conv_space, query_feats)
    sent_two, other_one = lax.optimization_barrier((sent_two, other_one))
    got_two = exchange(sent_two)
    other_two = from_neighbour(got_two)
    second = second.reshape(part, (SPOTS + 1) * pitch, LANES)

    third, sent = pl.pallas_call(
        functools.partial(expand_kernel, shares[2]),
        out_shape=(
            jax.ShapeDtypeStruct((wide, rows, LANES), jnp.float32),
            jax.ShapeDtypeStruct(
                (devices, 2 * part + wide + clips * len(shares[2]), LANES), jnp.bfloat16
            ),
        ),
        in_specs=[VMEM] * 7,
        out_specs=(VMEM, VMEM),
        scratch_shapes=[pltpu.VMEM((rows, inner), jnp.bfloat16)],
        compiler_params=pltpu.CompilerParams(vmem_limit_bytes=8 * MIB),
        name="expand",
    )(sent_two, got_two, row(gain_two), row(shift_two), second, conv_expand, query_feats)
    sent, other_two = lax.optimization_barrier((sent, other_two))
    got_three = exchange(sent)
    other_three = from_neighbour(got_three)

    own_keys, sent = pl.pallas_call(
        functools.partial(keys_kernel, lax.axis_size("bn")),
        out_shape=(
            jax.ShapeDtypeStruct((clips, emb), jnp.bfloat16),
            jax.ShapeDtypeStruct((devices, clips, emb), jnp.bfloat16),
        ),
        in_specs=[VMEM] * 12,
        out_specs=(VMEM, VMEM),
        scratch_shapes=[
            pltpu.VMEM((clips, channels), jnp.float32),
            pltpu.VMEM((2 * clips, queue.shape[0] // clips), jnp.float32),
        ],
        compiler_params=pltpu.CompilerParams(vmem_limit_bytes=8 * MIB),
        name="keys",
    )(
        sent_one,
        got_one,
        got_three,
        row(gain_three),
        row(shift_three),
        conv_expand,
        third,
        w_key,
        frames,
        query_feats,
        w_query,
        queue,
    )
    sent, other_three = lax.optimization_barrier((sent, other_three))
    query_grad = pl.pallas_call(
        functools.partial(gradient_kernel, shares),
        out_shape=jax.ShapeDtypeStruct((channels, emb), jnp.float32),
        in_specs=[VMEM] * 7,
        out_specs=ANY,
        scratch_shapes=[
            pltpu.VMEM((2, channels // 2, emb), jnp.float32),
            pltpu.SemaphoreType.DMA((2,)),
        ],
        compiler_params=pltpu.CompilerParams(vmem_limit_bytes=8 * MIB),
        name="query_grad",
    )(exchange(sent), got_one, got_two, got_three, other_one, other_two, other_three)
    return (own_keys, query_grad)


def solution(mesh):
    both = ("dp", "bn")
    placed = (
        P(both, None, None, None),
        P(both),
        P("bn", None),
        P(both, None),
    ) + (P(),) * 12
    return jax.shard_map(
        local, mesh=mesh, in_specs=placed, out_specs=(P(both, None), P()), check_vma=False
    )
```
